128 devices in a mesh: row: 16 (over y_lo, x, core), col: 8 (over y_hi, z).
Axes of the slice: x: 4, y: 4 (y_hi: 2, y_lo: 2; y = y_hi * 2 + y_lo), z: 4, core: 2. Of those that a mesh axis runs over, the one named last changes fastest.
Arguments:
- pair_repr: bfloat16 [896, 896, 128], P('row', 'col'), may hold values from -6 to 6
- residue_mask: int32 [896], replicated, may hold values 0 or 1
- chain_index: int32 [896], replicated, may hold values from 0 to 3, never falling along the last dimension, each value on 1 to 448 neighbouring positions
- chain_embed: float32 [2, 128], replicated, may hold values from -4 to 4
- outgoing_ab: bfloat16 [128, 512], replicated, may hold values from -0.5 to 0.5
- outgoing_gate: bfloat16 [128, 128], replicated, may hold values from -0.5 to 0.5
- outgoing_final: bfloat16 [128, 128], replicated, may hold values from -0.5 to 0.5
- incoming_ab: bfloat16 [128, 512], replicated, may hold values from -0.5 to 0.5
- incoming_gate: bfloat16 [128, 128], replicated, may hold values from -0.5 to 0.5
- incoming_final: bfloat16 [128, 128], replicated, may hold values from -0.5 to 0.5
Outputs:
- pair_out: bfloat16 [896, 896, 128], P('row', 'col')
The draws below stay inside these ranges and needn't reach their ends.
Inputs may be any that keep to these rules, and one draw needn't show every extreme that they name: `chain_index`: chain indices never fall along the residues; every chain has at least one residue and one chain has exactly 448.
All inputs are finite; a program needn't handle non-finite values.
Results may differ from the reference program's by a relative error of at most 0.0035.
Values may be sent and summed in bfloat16 or wider, within the bound.
A program may use at most 64 MiB of HBM per device.

```python
import math
import jax
import jax.numpy as jnp
import numpy as np
from jax import lax

C = 128
CH = 128
N = 896
NCHAIN = 4
N_ROW = 16


def place_ends(values, key, low, top_value):
    index_at = [jax.random.randint(jax.random.fold_in(key, axis), (), 0, length) for axis, length in enumerate(values.shape)]
    main_axis = values.shape.index(max(values.shape))
    next_to = index_at[:main_axis] + [(index_at[main_axis] + 1) % values.shape[main_axis]] + index_at[main_axis + 1:]
    return values.at[tuple(index_at)].set(low).at[tuple(next_to)].set(top_value)


def block_scale(stream_key, dims, split, least, top_value):
    level = 1.0
    for position, shards_of in split:
        heights = jax.random.uniform(jax.random.fold_in(jax.random.fold_in(stream_key, 6), position), (shards_of,), jnp.float32, least / len(split), top_value / len(split))
        level = level * jnp.repeat(jnp.exp(heights), dims[position] // shards_of).reshape((-1,) + (1,) * (len(dims) - 1 - position))
    return level


def split_up(count, total, most, skew):
    loads = [(1 << 20) // math.isqrt(grade ** skew) + 1 for grade in range(2, count + 1)]
    rest, given = total - most - (count - 1), [1] * (count - 1)
    while rest > 0:
        movable = [i for i in range(count - 1) if given[i] < most]
        whole, budget = sum([loads[i] for i in movable]), rest
        for i in movable:
            addition = min(most - given[i], max(1, budget * loads[i] // whole), rest)
            given[i] = given[i] + addition
            rest = rest - addition
    return np.array([most] + given)


def ragged(key, number_of, total, limit, slope):
    if number_of == 2:
        one = jax.random.randint(key, (), max(1, total - limit), min(limit, total - 1) + 1)
        return jnp.stack([one, total - one])
    tallies = jnp.asarray(split_up(number_of, total, limit, slope), jnp.int32)
    twos = (number_of - 1) // 2
    source_of, taker = tallies[1:1 + 2 * twos:2], tallies[2:2 + 2 * twos:2]
    slack = jnp.minimum(source_of - 1, limit - taker)
    moved = jax.random.randint(jax.random.fold_in(key, 1), (twos,), 0, 1 << 20) % (slack + 1)
    tallies = tallies.at[1:1 + 2 * twos:2].set(source_of - moved).at[2:2 + 2 * twos:2].set(taker + moved)
    return tallies[jax.random.permutation(jax.random.fold_in(key, 2), number_of)]


def normal_values(key, shape, deviation, bound, split=(), dtype=jnp.bfloat16):
    drawn = deviation * jax.random.normal(key, shape, jnp.float32)
    if split:
        drawn = drawn * block_scale(key, shape, split, -0.22, 0.18)
    return jnp.clip(drawn, -bound, bound).astype(dtype)


def setup_inputs(seed: int = 0) -> dict:
    seeds = jax.random.split(jax.random.key(seed), 11)
    pair_repr = normal_values(seeds[0], (N, N, C), 1.0, 6.0, ((0, 16), (1, 8)))
    residue_mask = place_ends((jax.random.randint(seeds[1], (N,), 0, 8) < 7).astype(jnp.int32), jax.random.fold_in(seeds[1], 1), 0, 1)
    chain_index = jnp.searchsorted(jnp.cumsum(ragged(seeds[2], NCHAIN, N, N // 2, 0)), jnp.arange(N), side="right").astype(jnp.int32)
    chain_embed = normal_values(seeds[3], (2, C), 1.0, 4.0, (), jnp.float32)
    outgoing_ab = normal_values(seeds[4], (C, 4 * CH), C ** -0.5, 0.5)
    outgoing_gate = normal_values(seeds[5], (C, C), C ** -0.5, 0.5)
    outgoing_final = normal_values(seeds[6], (CH, C), CH ** -0.5, 0.5)
    incoming_ab = normal_values(seeds[7], (C, 4 * CH), C ** -0.5, 0.5)
    incoming_gate = normal_values(seeds[8], (C, C), C ** -0.5, 0.5)
    incoming_final = normal_values(seeds[9], (CH, C), CH ** -0.5, 0.5)
    return {"pair_repr": pair_repr, "residue_mask": residue_mask, "chain_index": chain_index, "chain_embed": chain_embed, "outgoing_ab": outgoing_ab, "outgoing_gate": outgoing_gate, "outgoing_final": outgoing_final, "incoming_ab": incoming_ab, "incoming_gate": incoming_gate, "incoming_final": incoming_final}


EPSILON = 1e-05

def layer_norm(values, reduce_axes):
    center = values - lax.optimization_barrier(jnp.mean(values, axis=reduce_axes, keepdims=True))
    spread = lax.optimization_barrier(jnp.mean(center * center, axis=reduce_axes, keepdims=True))
    return center * lax.rsqrt(spread + EPSILON)

def triangle(pair_state, mask_float, w_ab, w_gate, w_final, incoming):
    band_rows = N // N_ROW
    band_count = N_ROW
    state_blocks = pair_state.reshape(band_count, band_rows, N, C)
    mask_blocks = mask_float.reshape(band_count, band_rows)

    def project(inputs):
        state_block, block_mask = inputs
        normed = layer_norm(state_block, (-1,)).astype(jnp.bfloat16)
        projected = jnp.einsum('ijc,ce->eij', normed.astype(jnp.float32), w_ab.astype(jnp.float32))
        pair_mask = block_mask[:, None] * mask_float[None, :]
        left_op = (jax.nn.sigmoid(projected[:CH]) * projected[CH:2 * CH] * pair_mask).astype(jnp.bfloat16)
        right_op = (jax.nn.sigmoid(projected[2 * CH:3 * CH]) * projected[3 * CH:] * pair_mask).astype(jnp.bfloat16)
        return (left_op, right_op)
    left_all, right_all = lax.map(project, (state_blocks, mask_blocks))
    left_all = jnp.moveaxis(left_all, 0, 1).reshape(CH, N, N)
    right_all = jnp.moveaxis(right_all, 0, 1).reshape(CH, N, N)

    def multiply(inputs):
        left_part, right_part = inputs
        left_part = left_part.astype(jnp.float32)
        right_part = right_part.astype(jnp.float32)
        if incoming:
            result = jnp.einsum('cki,ckj->cij', left_part, right_part)
        else:
            result = jnp.einsum('cik,cjk->cij', left_part, right_part)
        return result.astype(jnp.bfloat16)
    product = lax.map(multiply, (left_all.reshape(CH // 8, 8, N, N), right_all.reshape(CH // 8, 8, N, N)))
    product = product.reshape(CH, N, N)
    product_blocks = jnp.moveaxis(product.reshape(CH, band_count, band_rows, N), 1, 0)

    def finish(inputs):
        state_block, product_block = inputs
        normed = layer_norm(state_block, (-1,)).astype(jnp.bfloat16)
        gating = jax.nn.sigmoid(jnp.einsum('ijc,cd->ijd', normed.astype(jnp.float32), w_gate.astype(jnp.float32)))
        mixed_norm = layer_norm(jnp.moveaxis(product_block.astype(jnp.float32), 0, -1), (-1,)).astype(jnp.bfloat16)
        update = jnp.einsum('ije,ed->ijd', mixed_norm.astype(jnp.float32), w_final.astype(jnp.float32))
        return state_block + gating * update
    return lax.map(finish, (state_blocks, product_blocks)).reshape(N, N, C)

def reference(pair_repr, residue_mask, chain_index, chain_embed, outgoing_ab, outgoing_gate, outgoing_final, incoming_ab, incoming_gate, incoming_final):
    mask_float = residue_mask.astype(jnp.float32)
    same_chain = chain_index[:, None] == chain_index[None, :]
    pair_state = pair_repr.astype(jnp.float32) + jnp.where(same_chain[:, :, None], chain_embed[1], chain_embed[0])
    pair_state = triangle(pair_state, mask_float, outgoing_ab, outgoing_gate, outgoing_final, False)
    pair_state = triangle(pair_state, mask_float, incoming_ab, incoming_gate, incoming_final, True)
    return pair_state.astype(jnp.bfloat16)
```

```python
import jax
import jax.numpy as jnp
from jax import lax
from jax.experimental import pallas as pl
from jax.experimental.pallas import tpu as pltpu
from jax.sharding import PartitionSpec as P

EPSILON = 1e-05
MESH = pl.DeviceIdType.MESH
F32 = jnp.float32
BF16 = jnp.bfloat16

ROWS = 56
COLS = 112
LANES = 128
CH = 128
SKEW = 136


def peer(step, row, col):
    far = lax.rem(37 * step, 128)
    core = lax.rem(row + far, 2)
    x = lax.rem(row // 2 + far // 2, 4)
    z = lax.rem(col + far // 8, 4)
    y = lax.rem((col // 4) * 2 + row // 8 + far // 32, 4)
    return lax.rem(y, 2) * 8 + x * 2 + core, (y // 2) * 4 + z


def sigmoid(value):
    return 0.5 * jnp.tanh(0.5 * value) + 0.5


def kernel(
    x_ref, mask_ref, chain_ref, embed_ref,
    ab1_ref, gate1_ref, final1_ref, ab2_ref, gate2_ref, final2_ref,
    out_ref,
    state, normed, gating, stage, embed_t, ab_t, gate_t, final_t,
    left_out, right_out, prod_out, left_in, right_in, prod_in, left_panel, right_panel,
    send_sem, recv_sem, own_sem,
):
    row, col = lax.axis_index("row"), lax.axis_index("col")
    me = row * 8 + col
    barrier = pltpu.get_barrier_semaphore()

    def greet(step, carry):
        pl.semaphore_signal(barrier, inc=1, device_id=peer(step, row, col), device_id_type=MESH)
        return carry

    lax.fori_loop(1, 128, greet, 0)

    def turned(value):
        return value.astype(F32).T.astype(BF16)

    for update, (ab, gate, final) in enumerate(
        ((ab1_ref, gate1_ref, final1_ref), (ab2_ref, gate2_ref, final2_ref))
    ):
        for part in range(4):
            ab_t[update, part * CH : (part + 1) * CH, :] = turned(ab[:, part * CH : (part + 1) * CH])
        gate_t[update] = turned(gate[...])
        final_t[update] = turned(final[...])
    for kind in range(2):
        embed_t[kind] = jnp.broadcast_to(embed_ref[kind : kind + 1, :], (CH, CH)).T

    lane = lax.broadcasted_iota(jnp.int32, (1, LANES), 1)

    def collect(j, carry):
        mask, chain = carry
        here = lane == j
        mask = jnp.where(here, mask_ref[col * COLS + j].astype(F32), mask)
        return mask, jnp.where(here, chain_ref[col * COLS + j], chain)

    col_mask, col_chain = lax.fori_loop(
        0, COLS, collect, (jnp.zeros((1, LANES), F32), jnp.full((1, LANES), -1, jnp.int32))
    )

    def row_at(i):
        return pl.ds(pl.multiple_of(i * SKEW, 8), CH)

    def start_state(i):
        tile = jnp.concatenate([x_ref[i].astype(F32), jnp.zeros((LANES - COLS, CH), F32)], axis=0).T
        same = jnp.broadcast_to(col_chain == chain_ref[row * ROWS + i], (CH, LANES))
        return tile + jnp.where(same, embed_t[1], embed_t[0])

    def norm(value):
        center = value - jnp.sum(value, axis=0, keepdims=True) * (1.0 / CH)
        spread = jnp.sum(center * center, axis=0, keepdims=True) * (1.0 / CH)
        return (center * lax.rsqrt(spread + EPSILON)).astype(BF16)

    def operand(update, side, i, unit):
        weights = ab_t[update, side * 2 * CH : (side + 1) * 2 * CH, :]
        both = jnp.dot(weights, unit, preferred_element_type=F32)
        pair_mask = col_mask * mask_ref[row * ROWS + i].astype(F32)
        stage[row_at(i), :] = sigmoid(both[:CH]) * both[CH:] * pair_mask

    def exchange_start(source, target, where, number, row_to, col_to):
        pltpu.make_async_remote_copy(
            source, target.at[me], send_sem.at[number], recv_sem.at[number],
            device_id=(row_to, col_to), device_id_type=MESH,
        ).start()

    def relay(source, target, number):
        def gather(channel):
            source[channel] = stage[pl.ds(channel, ROWS, stride=SKEW), :].astype(BF16)

        def one(step, carry):
            row_to, col_to = peer(step, row, col)
            channel = row_to * 8 + col_to
            gather(channel)
            exchange_start(source.at[channel], target, None, number, row_to, col_to)
            return carry

        lax.fori_loop(1, 128, one, 0)
        gather(me)
        pltpu.make_async_copy(source.at[me], target.at[me], own_sem.at[number]).start()

    def arrive(source, target, number):
        pltpu.make_async_copy(source.at[me], target.at[me], own_sem.at[number]).wait()
        all_but_one = target.at[pl.ds(0, 127)]
        pltpu.make_async_copy(all_but_one, all_but_one, recv_sem.at[number]).wait()

    def sent(source, number):
        all_but_one = source.at[pl.ds(0, 127)]
        pltpu.make_async_copy(all_but_one, all_but_one, send_sem.at[number]).wait()

    for update in range(2):
        incoming = update == 1
        buffers = [b.at[update] for b in (left_out, right_out, prod_out, left_in, right_in, prod_in)]
        l_out, r_out, p_out, l_in, r_in, p_in = buffers
        base = update * 3

        def first(chunk, carry):
            for k in range(4):
                i = chunk * 4 + k
                if update == 0:
                    state[i] = start_state(i)
                else:
                    change = jnp.dot(final_t[0], stage[row_at(i), :].astype(BF16), preferred_element_type=F32)
                    state[i] = state[i] + gating[i] * change
                unit = norm(state[i])
                normed[i] = unit
                operand(update, 0, i, unit)
            return carry

        lax.fori_loop(0, ROWS // 4, first, 0)
        if update == 0:
            pl.semaphore_wait(barrier, 127)
        relay(l_out, l_in, base)

        def second(chunk, carry):
            for k in range(4):
                i = chunk * 4 + k
                operand(update, 1, i, normed[i])
            return carry

        lax.fori_loop(0, ROWS // 4, second, 0)
        relay(r_out, r_in, base + 1)

        def third(chunk, carry):
            for k in range(4):
                i = chunk * 4 + k
                gating[i] = sigmoid(jnp.dot(gate_t[update], normed[i], preferred_element_type=F32))
            return carry

        lax.fori_loop(0, ROWS // 4, third, 0)

        def panel(source, target, turn):
            def block(n, carry):
                high, low = n // 8, lax.rem(n, 8)
                tile = jnp.concatenate(
                    [
                        source[high * 16 + low].astype(F32),
                        source[high * 16 + 8 + low].astype(F32),
                        jnp.zeros((LANES - 2 * ROWS, LANES), F32),
                    ],
                    axis=0,
                )
                if turn:
                    high, low, tile = low, high, tile.T
                target[
                    pl.ds(pl.multiple_of(high * LANES, LANES), LANES),
                    pl.ds(pl.multiple_of(low * LANES, LANES), LANES),
                ] = tile.astype(BF16)
                return carry

            lax.fori_loop(0, 64, block, 0)

        arrive(l_out, l_in, base)
        panel(l_in, left_panel, incoming)
        arrive(r_out, r_in, base + 1)
        panel(r_in, right_panel, False)

        def multiply(n, carry):
            at = pl.ds(pl.multiple_of(n * 256, 256), 256)
            if incoming:
                part = jnp.dot(left_panel[...], right_panel[:, at], preferred_element_type=F32)
            else:
                part = lax.dot_general(
                    left_panel[...], right_panel[at, :], (((1,), (1,)), ((), ())), preferred_element_type=F32
                )
            for r in range(16):
                top = (r // 2) * LANES + (r % 2) * ROWS
                for s in range(2):
                    p_out[r * 8 + n * 2 + s] = part[top : top + ROWS, s * LANES : (s + 1) * LANES].astype(BF16)
            return carry

        lax.fori_loop(0, 4, multiply, 0)

        def give(step, carry):
            row_to, col_to = peer(step, row, col)
            exchange_start(p_out.at[row_to * 8 + col_to], p_in, None, base + 2, row_to, col_to)
            return carry

        lax.fori_loop(1, 128, give, 0)
        pltpu.make_async_copy(p_out.at[me], p_in.at[me], own_sem.at[base + 2]).start()
        arrive(p_out, p_in, base + 2)

        def add(c, total):
            return total + p_in[c].astype(F32)

        mean = lax.fori_loop(0, CH, add, jnp.zeros((ROWS, LANES), F32), unroll=8) * (1.0 / CH)

        def add_square(c, total):
            center = p_in[c].astype(F32) - mean
            return total + center * center

        spread = lax.fori_loop(0, CH, add_square, jnp.zeros((ROWS, LANES), F32), unroll=8) * (1.0 / CH)
        scale = lax.rsqrt(spread + EPSILON)

        def spread_out(c, carry):
            stage[pl.ds(c, ROWS, stride=SKEW), :] = (p_in[c].astype(F32) - mean) * scale
            return carry

        lax.fori_loop(0, CH, spread_out, 0, unroll=8)

    def last(chunk, carry):
        for k in range(4):
            i = chunk * 4 + k
            change = jnp.dot(final_t[1], stage[row_at(i), :].astype(BF16), preferred_element_type=F32)
            value = state[i] + gating[i] * change
            out_ref[i] = value.T[:COLS].astype(BF16)
        return carry

    lax.fori_loop(0, ROWS // 4, last, 0)
    for update in range(2):
        for number, source in enumerate((left_out, right_out, prod_out)):
            sent(source.at[update], update * 3 + number)


def body(*args):
    vmem, smem = (pl.BlockSpec(memory_space=m) for m in (pltpu.VMEM, pltpu.SMEM))
    tiles = pltpu.VMEM((2, CH, ROWS, LANES), BF16)
    return pl.pallas_call(
        kernel,
        out_shape=jax.ShapeDtypeStruct((ROWS, COLS, CH), BF16),
        in_specs=[vmem, smem, smem] + [vmem] * 7,
        out_specs=vmem,
        scratch_shapes=[
            pltpu.VMEM((ROWS, CH, LANES), F32),
            pltpu.VMEM((ROWS, CH, LANES), BF16),
            pltpu.VMEM((ROWS, CH, LANES), F32),
            pltpu.VMEM((ROWS * SKEW, LANES), F32),
            pltpu.VMEM((2, CH, LANES), F32),
            pltpu.VMEM((2, 4 * CH, CH), BF16),
            pltpu.VMEM((2, CH, CH), BF16),
            pltpu.VMEM((2, CH, CH), BF16),
            tiles, tiles, tiles, tiles, tiles, tiles,
            pltpu.VMEM((8 * LANES, 8 * LANES), BF16),
            pltpu.VMEM((8 * LANES, 8 * LANES), BF16),
            pltpu.SemaphoreType.DMA((6,)),
            pltpu.SemaphoreType.DMA((6,)),
            pltpu.SemaphoreType.DMA((6,)),
        ],
        compiler_params=pltpu.CompilerParams(
            collective_id=0, has_side_effects=True, vmem_limit_bytes=62 << 20
        ),
    )(*args)


def solution(mesh):
    in_specs = (P("row", "col", None), P(), P(), P(), P(), P(), P(), P(), P(), P())
    out_specs = P("row", "col", None)
    return jax.shard_map(body, mesh=mesh, in_specs=in_specs, out_specs=out_specs, check_vma=False)
```

```python
import jax
import jax.numpy as jnp
from jax import lax
from jax.experimental import pallas as pl
from jax.experimental.pallas import tpu as pltpu
from jax.sharding import PartitionSpec as P

EPSILON = 1e-05
MESH = pl.DeviceIdType.MESH
F32 = jnp.float32
BF16 = jnp.bfloat16

ROWS = 56
COLS = 112
LANES = 128
CH = 128
SKEW = 136
HALVES = ((0, 32), (32, 24))
WIDE = 256


def peer(step, row, col):
    far = lax.rem(37 * step, 128)
    core = lax.rem(row + far, 2)
    x = lax.rem(row // 2 + far // 2, 4)
    z = lax.rem(col + far // 8, 4)
    y = lax.rem((col // 4) * 2 + row // 8 + far // 32, 4)
    return lax.rem(y, 2) * 8 + x * 2 + core, (y // 2) * 4 + z


def sigmoid(value):
    return 0.5 * jnp.tanh(0.5 * value) + 0.5


def for_each_peer(one):
    def turn(n, carry):
        for k in range(4):
            one(1 + n * 4 + k)
        return carry

    lax.fori_loop(0, 31, turn, 0)
    for step in range(125, 128):
        one(step)


def kernel(
    x_ref, mask_ref, chain_ref, embed_ref,
    ab1_ref, gate1_ref, final1_ref, ab2_ref, gate2_ref, final2_ref,
    out_ref,
    state, normed, gating, stage, embed_t, ab_t, gate_t, final_t, left_panel, right_panel, total,
    out_a, out_b, in_a, in_b,
    send_sem, recv_sem,
):
    row, col = lax.axis_index("row"), lax.axis_index("col")
    me = row * 8 + col
    barrier = pltpu.get_barrier_semaphore()

    def greet(step):
        pl.semaphore_signal(barrier, inc=1, device_id=peer(step, row, col), device_id_type=MESH)

    for_each_peer(greet)

    def turned(value):
        return value.astype(F32).T.astype(BF16)

    for update, (ab, gate, final) in enumerate(
        ((ab1_ref, gate1_ref, final1_ref), (ab2_ref, gate2_ref, final2_ref))
    ):
        for part in range(4):
            ab_t[update, part * CH : (part + 1) * CH, :] = turned(ab[:, part * CH : (part + 1) * CH])
        gate_t[update] = turned(gate[...])
        final_t[update] = turned(final[...])
    for kind in range(2):
        embed_t[kind] = jnp.broadcast_to(embed_ref[kind : kind + 1, :], (CH, CH)).T

    lane = lax.broadcasted_iota(jnp.int32, (1, LANES), 1)

    def collect(j, carry):
        mask, chain = carry
        here = lane == j
        mask = jnp.where(here, mask_ref[col * COLS + j].astype(F32), mask)
        return mask, jnp.where(here, chain_ref[col * COLS + j], chain)

    col_mask, col_chain = lax.fori_loop(
        0, COLS, collect, (jnp.zeros((1, LANES), F32), jnp.full((1, LANES), -1, jnp.int32)), unroll=8
    )

    def row_at(i):
        return pl.ds(pl.multiple_of(i * SKEW, 8), CH)

    def start_state(i):
        tile = jnp.concatenate([x_ref[i].astype(F32), jnp.zeros((LANES - COLS, CH), F32)], axis=0).T
        same = jnp.broadcast_to(col_chain == chain_ref[row * ROWS + i], (CH, LANES))
        return tile + jnp.where(same, embed_t[1], embed_t[0])

    def norm(value):
        center = value - jnp.sum(value, axis=0, keepdims=True) * (1.0 / CH)
        spread = jnp.sum(center * center, axis=0, keepdims=True) * (1.0 / CH)
        return (center * lax.rsqrt(spread + EPSILON)).astype(BF16)

    def operand(update, side, rows, units):
        weights = ab_t[update, side * 2 * CH : (side + 1) * 2 * CH, :]
        both = jnp.dot(weights, jnp.concatenate(units, axis=1), preferred_element_type=F32)
        for k, i in enumerate(rows):
            pair_mask = col_mask * mask_ref[row * ROWS + i].astype(F32)
            one = both[:, k * LANES : (k + 1) * LANES]
            stage[row_at(i), :] = sigmoid(one[:CH]) * one[CH:] * pair_mask

    def for_rows(half, several, visit):
        begin, count = HALVES[half]

        def turn(n, carry):
            visit([begin + n * several + k for k in range(several)])
            return carry

        lax.fori_loop(0, count // several, turn, 0)

    LEFT, RIGHT, PRODUCT = 0, 1, 2
    outs, ins = (out_a, out_b), (in_a, in_b)

    def slot(update, kind, half):
        return (update * 3 + kind) * 2 + half

    def send(update, kind, half, row_to, col_to):
        number = slot(update, kind, half)
        pltpu.make_async_remote_copy(
            outs[half].at[update * 3 + kind, row_to * 8 + col_to], ins[half].at[update * 3 + kind, me],
            send_sem.at[number], recv_sem.at[number], device_id=(row_to, col_to), device_id_type=MESH,
        ).start()

    def relay(update, kind, half):
        begin, count = HALVES[half]

        def gather(channel):
            return stage[pl.ds(begin * SKEW + channel, count, stride=SKEW), :].astype(BF16)

        def one(step):
            row_to, col_to = peer(step, row, col)
            channel = row_to * 8 + col_to
            outs[half][update * 3 + kind, channel] = gather(channel)
            send(update, kind, half, row_to, col_to)

        for_each_peer(one)
        ins[half][update * 3 + kind, me] = gather(me)

    def arrive(update, kind, half):
        others = ins[half].at[update * 3 + kind, pl.ds(0, 127)]
        pltpu.make_async_copy(others, others, recv_sem.at[slot(update, kind, half)]).wait()

    def give(update, half):
        def one(step):
            row_to, col_to = peer(step, row, col)
            send(update, PRODUCT, half, row_to, col_to)

        for_each_peer(one)
        ins[half][update * 3 + PRODUCT, me] = outs[half][update * 3 + PRODUCT, me]

    def columns(visit):
        def turn(s, carry):
            visit(s, pl.ds(pl.multiple_of(s * LANES, LANES), LANES))
            return carry

        lax.fori_loop(0, 8, turn, 0)

    def received(update, kind, half, s):
        return [ins[half][update * 3 + kind, r * 8 + s].astype(F32) for r in range(16)]

    def plain_panel(update, kind, half, panel, first):
        count = HALVES[half][1]

        def visit(s, at):
            tiles = jnp.concatenate(received(update, kind, half, s), axis=0)
            panel[first : first + 16 * count, at] = tiles.astype(BF16)

        columns(visit)

    def turned_panel(update, kind, half, panel, first):
        count = HALVES[half][1]

        def visit(s, at):
            tiles = jnp.concatenate(received(update, kind, half, s), axis=0)
            panel[at, first : first + 16 * count] = tiles.T.astype(BF16)

        columns(visit)

    def padded_panel(update, kind, panel):
        def visit(s, at):
            one, two = received(update, kind, 0, s), received(update, kind, 1, s)
            nothing = jnp.zeros((LANES - 2 * ROWS, LANES), F32)
            for a in range(8):
                pieces = [one[2 * a], two[2 * a], one[2 * a + 1], two[2 * a + 1], nothing]
                panel[a * LANES : (a + 1) * LANES, at] = jnp.concatenate(pieces, axis=0).astype(BF16)

        columns(visit)

    def wide(visit):
        def turn(n, carry):
            visit(n, pl.ds(pl.multiple_of(n * WIDE, WIDE), WIDE))
            return carry

        lax.fori_loop(0, 8 * LANES // WIDE, turn, 0)

    def outgoing_product(half, first):
        count = HALVES[half][1]

        def visit(n, at):
            part = lax.dot_general(
                left_panel[first : first + 16 * count, :], right_panel[at, :], (((1,), (1,)), ((), ())),
                preferred_element_type=F32,
            )
            for r in range(16):
                for k in range(WIDE // LANES):
                    block = part[r * count : (r + 1) * count, k * LANES : (k + 1) * LANES]
                    outs[half][PRODUCT, r * 8 + n * (WIDE // LANES) + k] = block.astype(BF16)

        wide(visit)

    def incoming_first(depth):
        def visit(n, at):
            total[:, at] = jnp.dot(left_panel[:, :depth], right_panel[:depth, at], preferred_element_type=F32)

        wide(visit)

    def incoming_second(begin, end):
        def visit(n, at):
            part = total[:, at] + jnp.dot(
                left_panel[:, begin:end], right_panel[begin:end, at], preferred_element_type=F32
            )
            for r in range(16):
                for half, (top, count) in enumerate(HALVES):
                    top = (r // 2) * LANES + (r % 2) * ROWS + top
                    for k in range(WIDE // LANES):
                        block = part[top : top + count, k * LANES : (k + 1) * LANES]
                        outs[half][3 + PRODUCT, r * 8 + n * (WIDE // LANES) + k] = block.astype(BF16)

        wide(visit)

    def mix(update, half):
        begin, count = HALVES[half]
        which = update * 3 + PRODUCT
        nothing = jnp.zeros((count, LANES), F32)

        def add(c, carry):
            return carry + ins[half][which, c].astype(F32)

        mean = lax.fori_loop(0, CH, add, nothing, unroll=8) * (1.0 / CH)

        def add_square(c, carry):
            center = ins[half][which, c].astype(F32) - mean
            return carry + center * center

        spread = lax.fori_loop(0, CH, add_square, nothing, unroll=8) * (1.0 / CH)
        scale = lax.rsqrt(spread + EPSILON)

        def put(c, carry):
            center = ins[half][which, c].astype(F32) - mean
            stage[pl.ds(begin * SKEW + c, count, stride=SKEW), :] = center * scale
            return carry

        lax.fori_loop(0, CH, put, 0, unroll=8)

    def changed(update, rows):
        mixed = jnp.concatenate([stage[row_at(i), :].astype(BF16) for i in rows], axis=1)
        change = jnp.dot(final_t[update], mixed, preferred_element_type=F32)
        return [
            state[i] + gating[i] * change[:, k * LANES : (k + 1) * LANES] for k, i in enumerate(rows)
        ]

    def first(update):
        def visit(rows):
            values = [start_state(i) for i in rows] if update == 0 else changed(0, rows)
            units = [norm(value) for value in values]
            for i, value, unit in zip(rows, values, units):
                state[i] = value
                normed[i] = unit
            operand(update, RIGHT, rows, units)

        return visit

    def second(update):
        def visit(rows):
            operand(update, LEFT, rows, [normed[i] for i in rows])

        return visit

    def third(update):
        def visit(rows):
            units = jnp.concatenate([normed[i] for i in rows], axis=1)
            gates = sigmoid(jnp.dot(gate_t[update], units, preferred_element_type=F32))
            for k, i in enumerate(rows):
                gating[i] = gates[:, k * LANES : (k + 1) * LANES]

        return visit

    def last(rows):
        for i, value in zip(rows, changed(1, rows)):
            out_ref[i] = value.T[:COLS].astype(BF16)

    for_rows(0, 4, first(0))
    pl.semaphore_wait(barrier, 127)
    relay(0, RIGHT, 0)
    for_rows(1, 4, first(0))
    relay(0, RIGHT, 1)
    for half in range(2):
        for_rows(half, 4, second(0))
        relay(0, LEFT, half)
    for half in range(2):
        for_rows(half, 4, third(0))
    arrive(0, RIGHT, 0)
    arrive(0, RIGHT, 1)
    padded_panel(0, RIGHT, right_panel)
    for half, place in ((0, 0), (1, 512)):
        arrive(0, LEFT, half)
        plain_panel(0, LEFT, half, left_panel, place)
        outgoing_product(half, place)
        give(0, half)

    for half in range(2):
        arrive(0, PRODUCT, half)
        mix(0, half)
        for_rows(half, 4, first(1))
        relay(1, RIGHT, half)
        for_rows(half, 4, second(1))
        relay(1, LEFT, half)
    for half in range(2):
        for_rows(half, 4, third(1))
    for half, place in ((0, 0), (1, 512)):
        arrive(1, RIGHT, half)
        plain_panel(1, RIGHT, half, right_panel, place)
        arrive(1, LEFT, half)
        turned_panel(1, LEFT, half, left_panel, place)
        if half == 0:
            incoming_first(512)
        else:
            incoming_second(512, 896)
    for half in range(2):
        give(1, half)
    for half in range(2):
        arrive(1, PRODUCT, half)
        mix(1, half)
        for_rows(half, 4, last)

    for update in range(2):
        for kind in range(3):
            for half in range(2):
                others = outs[half].at[update * 3 + kind, pl.ds(0, 127)]
                pltpu.make_async_copy(others, others, send_sem.at[slot(update, kind, half)]).wait()


def body(*args):
    vmem, smem = (pl.BlockSpec(memory_space=m) for m in (pltpu.VMEM, pltpu.SMEM))
    tiles_a = pltpu.VMEM((6, CH, HALVES[0][1], LANES), BF16)
    tiles_b = pltpu.VMEM((6, CH, HALVES[1][1], LANES), BF16)
    return pl.pallas_call(
        kernel,
        out_shape=jax.ShapeDtypeStruct((ROWS, COLS, CH), BF16),
        in_specs=[vmem, smem, smem] + [vmem] * 7,
        out_specs=vmem,
        scratch_shapes=[
            pltpu.VMEM((ROWS, CH, LANES), F32),
            pltpu.VMEM((ROWS, CH, LANES), BF16),
            pltpu.VMEM((ROWS, CH, LANES), F32),
            pltpu.VMEM((ROWS * SKEW, LANES), F32),
            pltpu.VMEM((2, CH, LANES), F32),
            pltpu.VMEM((2, 4 * CH, CH), BF16),
            pltpu.VMEM((2, CH, CH), BF16),
            pltpu.VMEM((2, CH, CH), BF16),
            pltpu.VMEM((8 * LANES, 8 * LANES), BF16),
            pltpu.VMEM((8 * LANES, 8 * LANES), BF16),
            pltpu.VMEM((8 * LANES, 8 * LANES), F32),
            tiles_a, tiles_b, tiles_a, tiles_b,
            pltpu.SemaphoreType.DMA((12,)),
            pltpu.SemaphoreType.DMA((12,)),
        ],
        compiler_params=pltpu.CompilerParams(
            collective_id=0, has_side_effects=True, vmem_limit_bytes=62 << 20
        ),
    )(*args)


def solution(mesh):
    in_specs = (P("row", "col", None), P(), P(), P(), P(), P(), P(), P(), P(), P())
    out_specs = P("row", "col", None)
    return jax.shard_map(body, mesh=mesh, in_specs=in_specs, out_specs=out_specs, check_vma=False)
```

```python
import jax
import jax.numpy as jnp
from jax import lax
from jax.experimental import pallas as pl
from jax.experimental.pallas import tpu as pltpu
from jax.sharding import PartitionSpec as P

EPSILON = 1e-05
MESH = pl.DeviceIdType.MESH
F32 = jnp.float32
BF16 = jnp.bfloat16

ROWS = 56
COLS = 112
LANES = 128
TILES = 49
CH = 128
GROUP = 8
SHIFT = LANES - COLS
SKEW = 136
WIDE = 256
FIRST = 24
RA, RB, LA, LB, LX, PA, PB, PX = range(8)
MESSAGES = (24, 24, 32, 16, 2, 24, 24, 2) + (24, 24, 24, 24, 2, 24, 24, 2)


def peer(step, row, col):
    far = lax.rem(37 * step, 128)
    core = lax.rem(row + far, 2)
    x = lax.rem(row // 2 + far // 2, 4)
    z = lax.rem(col + far // 8, 4)
    y = lax.rem((col // 4) * 2 + row // 8 + far // 32, 4)
    return lax.rem(y, 2) * 8 + x * 2 + core, (y // 2) * 4 + z


def sigmoid(value):
    return 0.5 * jnp.tanh(0.5 * value) + 0.5


def for_each_peer(one):
    def turn(n, carry):
        for k in range(4):
            one(1 + n * 4 + k)
        return carry

    lax.fori_loop(0, 31, turn, 0)
    for step in range(125, 128):
        one(step)


def kernel(
    x_hbm, mask_ref, chain_ref, embed_ref,
    ab1_ref, gate1_ref, final1_ref, ab2_ref, gate2_ref, final2_ref,
    out_ref,
    x_ref, state, normed, gating, stage, pair_mask, same_chain, embed_t, ab_t, gate_t, final_t,
    left_panel, right_panel, total, spare, kept, products, flat, flat_product,
    *rest,
):
    outs, ins = rest[:16], rest[16:32]
    send_sem, recv_sem, x_sem = rest[32:]
    row, col = lax.axis_index("row"), lax.axis_index("col")
    me = row * 8 + col
    barrier = pltpu.get_barrier_semaphore()

    def greet(row_to, col_to):
        pl.semaphore_signal(barrier, inc=1, device_id=(row_to, col_to), device_id_type=MESH)

    def greet_row(n, carry):
        for k in range(8):
            greet(lax.rem(row + n, 16), k)
        return carry

    for k in range(1, 8):
        greet(row, lax.rem(col + k, 8))
    lax.fori_loop(1, 16, greet_row, 0)
    x_copies = []
    for number, (begin, end) in enumerate(((0, FIRST * LANES), (FIRST * LANES, TILES * LANES))):
        at = pl.ds(begin, end - begin)
        x_copies.append(pltpu.make_async_copy(x_hbm.at[at], x_ref.at[at], x_sem.at[number]))
        x_copies[number].start()

    def turned(value):
        return value.astype(F32).T.astype(BF16)

    def turn_ab(update, ab, side):
        for part in (2 * side, 2 * side + 1):
            ab_t[update, part * CH : (part + 1) * CH, :] = turned(ab[:, part * CH : (part + 1) * CH])

    lane = lax.broadcasted_iota(jnp.int32, (1, LANES), 1)

    def collect(j, carry):
        mask, chain = carry
        here = lane == j
        mask = jnp.where(here, mask_ref[col * COLS + j], mask)
        return mask, jnp.where(here, chain_ref[col * COLS + j], chain)

    nothing = jnp.zeros((1, LANES), jnp.int32)
    col_mask, col_chain = lax.fori_loop(0, COLS, collect, (nothing, nothing), unroll=8)
    for phase in range(7):
        skip = SHIFT * phase

        def wrapped(value):
            value = value.astype(F32)
            near = pltpu.roll(value, LANES - skip, 1) if skip else value
            return jnp.where(lane < COLS - skip, near, pltpu.roll(value, COLS - skip, 1))

        tile_mask, tile_chain = wrapped(col_mask), wrapped(col_chain)
        for t in range(phase, TILES, 7):
            i = row * ROWS + t + t // 7
            near = lane < COLS - skip
            own_mask = jnp.where(near, mask_ref[i].astype(F32), mask_ref[i + 1].astype(F32))
            own_chain = jnp.where(near, chain_ref[i].astype(F32), chain_ref[i + 1].astype(F32))
            pair_mask[t : t + 1, :] = tile_mask * own_mask
            same_chain[t : t + 1, :] = jnp.where(tile_chain == own_chain, 1.0, 0.0)
    flat[...] = jnp.zeros(flat.shape, F32)

    lanes = lax.broadcasted_iota(jnp.int32, (GROUP, LANES), 1)
    row_of = lax.broadcasted_iota(jnp.int32, (GROUP, LANES), 0)
    from_former = lanes >= LANES - SHIFT * row_of
    from_same = lanes < COLS - SHIFT * row_of
    turn_back = (lanes + SHIFT * row_of) % LANES

    def unfold(tiles):
        mixed = jnp.where(from_former, pltpu.roll(tiles, 1, 0), tiles)
        return pltpu.roll(mixed, 0, 1, stride=SHIFT, stride_axis=0)

    def fold(rows):
        moved = jnp.take_along_axis(rows, turn_back, axis=1, mode="promise_in_bounds")
        return jnp.where(from_same, moved, pltpu.roll(moved, GROUP - 1, 0))

    def tile_at(t):
        return pl.ds(pl.multiple_of(t * SKEW, 8), CH)

    def positions(t):
        return pl.ds(pl.multiple_of(t * LANES, LANES), LANES)

    def start_state(t):
        same = jnp.broadcast_to(same_chain[pl.ds(t, 1), :], (CH, LANES)) > 0.5
        return x_ref[positions(t), :].astype(F32).T + jnp.where(same, embed_t[1], embed_t[0])

    def norm(value):
        center = value - jnp.sum(value, axis=0, keepdims=True) * (1.0 / CH)
        spread = jnp.sum(center * center, axis=0, keepdims=True) * (1.0 / CH)
        return (center * lax.rsqrt(spread + EPSILON)).astype(BF16)

    def operand(update, side, tiles, units):
        weights = ab_t[update, side * 2 * CH : (side + 1) * 2 * CH, :]
        both = jnp.dot(weights, jnp.concatenate(units, axis=1), preferred_element_type=F32)
        for k, t in enumerate(tiles):
            one = both[:, k * LANES : (k + 1) * LANES]
            stage[tile_at(t), :] = sigmoid(one[:CH]) * one[CH:] * pair_mask[pl.ds(t, 1), :]

    def for_tiles(begin, end, visit):
        def turn(n, carry):
            visit([begin + n * 4 + k for k in range(4)])
            return carry

        turns = (end - begin) // 4
        lax.fori_loop(0, turns, turn, 0)
        if begin + turns * 4 < end:
            visit(list(range(begin + turns * 4, end)))

    LEFT, RIGHT = 0, 1

    def send(number, row_to, col_to):
        pltpu.make_async_remote_copy(
            outs[number].at[row_to * 8 + col_to], ins[number].at[me],
            send_sem.at[number], recv_sem.at[number], device_id=(row_to, col_to), device_id_type=MESH,
        ).start()

    def staged(channel, begin, count):
        return stage[pl.ds(begin * SKEW + channel, count, stride=SKEW), :]

    def relay(make):
        def one(step):
            row_to, col_to = peer(step, row, col)
            channel = row_to * 8 + col_to
            for number, value in make(channel):
                outs[number][channel] = value.astype(BF16)
                send(number, row_to, col_to)

        for_each_peer(one)
        for number, value in make(me):
            ins[number][me] = value.astype(BF16)

    def arrive(*numbers):
        for number in numbers:
            others = ins[number].at[pl.ds(0, 127)]
            pltpu.make_async_copy(others, others, recv_sem.at[number]).wait()

    def give(*numbers):
        def one(step):
            row_to, col_to = peer(step, row, col)
            for number in numbers:
                send(number, row_to, col_to)

        for_each_peer(one)
        for number in numbers:
            ins[number][me] = outs[number][me]

    def got(number, source):
        return ins[number][source].astype(F32)

    def columns(visit):
        def turn(s, carry):
            visit(s, pl.ds(pl.multiple_of(s * LANES, LANES), LANES))
            return carry

        lax.fori_loop(0, 8, turn, 0)

    def wide(visit):
        def turn(n, carry):
            visit(n, pl.ds(pl.multiple_of(n * WIDE, WIDE), WIDE))
            return carry

        lax.fori_loop(0, 8 * LANES // WIDE, turn, 0)

    def unfolded(r, begin, end):
        return [unfold(flat[r, 7 * g : 7 * g + GROUP]) for g in range(begin, end)]

    def folded(slot, begin, rows):
        for g in range(rows.shape[0] // GROUP):
            at = 7 * (begin + g)
            flat_product[slot, at : at + GROUP] = fold(rows[g * GROUP : (g + 1) * GROUP])

    def mix(update, half):
        begin, count, padded = ((0, FIRST, FIRST), (FIRST, TILES - FIRST, 32))[half]
        pa, pb, px = (update * 8 + number for number in (PA, PB, PX))

        def add(c, carry):
            if half == 0:
                tile = got(pa, c)
            else:
                tile = jnp.concatenate([got(pb, c), jnp.broadcast_to(got(px, c)[0:1], (GROUP, LANES))], axis=0)
            products[c, :padded] = tile
            return carry + tile

        empty = jnp.zeros((padded, LANES), F32)
        mean = lax.fori_loop(0, CH, add, empty, unroll=8) * (1.0 / CH)

        def add_square(c, carry):
            center = products[c, :padded] - mean
            return carry + center * center

        spread = lax.fori_loop(0, CH, add_square, empty, unroll=8) * (1.0 / CH)
        scale = lax.rsqrt(spread + EPSILON)

        def put(c, carry):
            value = (products[c, :padded] - mean) * scale
            stage[pl.ds(begin * SKEW + c, count, stride=SKEW), :] = value[:count]
            return carry

        lax.fori_loop(0, CH, put, 0, unroll=8)

    def changed(update, tiles):
        mixed = jnp.concatenate([stage[tile_at(t), :].astype(BF16) for t in tiles], axis=1)
        change = jnp.dot(final_t[update], mixed, preferred_element_type=F32)
        return [
            state[t] + gating[t] * change[:, k * LANES : (k + 1) * LANES] for k, t in enumerate(tiles)
        ]

    def first(update):
        def visit(tiles):
            values = [start_state(t) for t in tiles] if update == 0 else changed(0, tiles)
            units = [norm(value) for value in values]
            for t, value, unit in zip(tiles, values, units):
                state[t] = value
                normed[t] = unit
            operand(update, RIGHT, tiles, units)

        return visit

    def second(update):
        def visit(tiles):
            operand(update, LEFT, tiles, [normed[t] for t in tiles])

        return visit

    def third(update):
        def visit(tiles):
            units = jnp.concatenate([normed[t] for t in tiles], axis=1)
            gates = sigmoid(jnp.dot(gate_t[update], units, preferred_element_type=F32))
            for k, t in enumerate(tiles):
                gating[t] = gates[:, k * LANES : (k + 1) * LANES]

        return visit

    def last(tiles):
        for t, value in zip(tiles, changed(1, tiles)):
            out_ref[positions(t), :] = value.T.astype(BF16)

    turn_ab(0, ab1_ref, RIGHT)
    for kind in range(2):
        embed_t[kind] = jnp.broadcast_to(embed_ref[kind : kind + 1, :], (CH, CH)).T
    x_copies[0].wait()
    for_tiles(0, FIRST, first(0))

    def right_first(channel):
        return [(RA, staged(channel, 0, FIRST))]

    def right_second(channel):
        spare[channel] = staged(channel, TILES - 1, 1)
        return [(RB, staged(channel, FIRST, 24))]

    def left_first(channel):
        tile = staged(channel, 0, 32)
        end = jnp.where(row_of == 7, jnp.broadcast_to(spare[channel], (GROUP, LANES)), tile[24:])
        return [(LA, jnp.concatenate([tile[:24], end], axis=0))]

    def left_second(channel):
        return [(LB, staged(channel, 31, 16)), (LX, staged(channel, 47, 2))]

    pl.semaphore_wait(barrier, 127)
    relay(right_first)
    x_copies[1].wait()
    for_tiles(FIRST, TILES, first(0))
    relay(right_second)
    turn_ab(0, ab1_ref, LEFT)
    for_tiles(0, TILES, second(0))
    relay(left_first)
    relay(left_second)
    for update, (gate, final) in enumerate(((gate1_ref, final1_ref), (gate2_ref, final2_ref))):
        gate_t[update] = turned(gate[...])
        final_t[update] = turned(final[...])
    for side in (LEFT, RIGHT):
        turn_ab(1, ab2_ref, side)
    for_tiles(0, TILES, third(0))

    def right_columns(s, at):
        empty = jnp.zeros((LANES - 2 * ROWS, LANES), F32)
        for r in range(16):
            source = r * 8 + s
            flat[r, 0:24] = got(RA, source)
            flat[r, 24:48] = got(RB, source)
            flat[r, 48:49] = got(LA, source)[31:32]
        for a in range(8):
            rows = unfolded(2 * a, 0, 7) + unfolded(2 * a + 1, 0, 7)
            rows = [jnp.where(lanes < COLS, part, 0.0) for part in rows]
            right_panel[a * LANES : (a + 1) * LANES, at] = jnp.concatenate(rows + [empty], axis=0).astype(BF16)

    def left_columns_first(s, at):
        rows = []
        for r in range(16):
            flat[r, 0:32] = got(LA, r * 8 + s)
            rows += unfolded(r, 0, 4)
        left_panel[:512, at] = jnp.concatenate(rows, axis=0).astype(BF16)

    def left_columns_second(s, at):
        rows = []
        for r in range(16):
            source = r * 8 + s
            flat[r, 24:32] = got(LA, source)[24:32]
            flat[r, 31:47] = got(LB, source)
            flat[r, 47:49] = got(LX, source)
            rows += unfolded(r, 4, 7)
        left_panel[512:896, at] = jnp.concatenate(rows, axis=0).astype(BF16)

    def outgoing_product(begin, end, half):
        count = (end - begin) // 16

        def visit(n, at):
            part = lax.dot_general(
                left_panel[begin:end, :], right_panel[at, :], (((1,), (1,)), ((), ())),
                preferred_element_type=F32,
            )
            for r in range(16):
                for k in range(WIDE // LANES):
                    block = part[r * count : (r + 1) * count, k * LANES : (k + 1) * LANES]
                    dest = r * 8 + n * (WIDE // LANES) + k
                    slot = r * 2 + k
                    if half == 0:
                        folded(slot, 0, block)
                        outs[PA][dest] = flat_product[slot, 0:24].astype(BF16)
                        kept[dest] = flat_product[slot, 24:32]
                    else:
                        flat_product[slot, 24:32] = kept[dest]
                        folded(slot, 4, block)
                        outs[PB][dest] = flat_product[slot, 24:48].astype(BF16)
                        outs[PX][dest] = flat_product[slot, 48:50].astype(BF16)

        wide(visit)

    arrive(RA, RB, LA)
    columns(right_columns)
    columns(left_columns_first)
    outgoing_product(0, 512, 0)
    give(PA)
    arrive(LB, LX)
    columns(left_columns_second)
    outgoing_product(512, 896, 1)
    give(PB, PX)

    def right_one(channel):
        return [(8 + RA, staged(channel, 0, FIRST))]

    def left_one(channel):
        return [(8 + LA, staged(channel, 0, FIRST))]

    def right_two(channel):
        spare[channel] = staged(channel, TILES - 1, 1)
        return [(8 + RB, staged(channel, FIRST, 24))]

    def left_two(channel):
        extra = jnp.concatenate([spare[channel], staged(channel, TILES - 1, 1)], axis=0)
        return [(8 + LB, staged(channel, FIRST, 24)), (8 + LX, extra)]

    arrive(PA)
    mix(0, 0)
    for_tiles(0, FIRST, first(1))
    relay(right_one)
    for_tiles(0, FIRST, second(1))
    relay(left_one)
    arrive(PB, PX)
    mix(0, 1)
    for_tiles(FIRST, TILES, first(1))
    relay(right_two)
    for_tiles(FIRST, TILES, second(1))
    relay(left_two)
    for_tiles(0, TILES, third(1))

    def incoming_columns(begin, end, numbers, turn):
        first_group, last_group = begin // GROUP, end // GROUP
        depth = pl.ds(16 * begin, 16 * (end - begin))

        def visit(s, at):
            rows = []
            for r in range(16):
                source = r * 8 + s
                flat[r, 0:24] = got(numbers[0], source)
                if end == ROWS:
                    flat[r, 24:48] = got(numbers[1], source)
                    extra = got(8 + LX, source)
                    flat[r, 48:49] = extra[1:2] if turn else extra[0:1]
                rows += unfolded(r, first_group, last_group)
            rows = jnp.concatenate(rows, axis=0)
            if turn:
                left_panel[at, depth] = rows.T.astype(BF16)
            else:
                right_panel[depth, at] = rows.astype(BF16)

        columns(visit)

    def incoming_first(n, at):
        total[:, at] = jnp.dot(left_panel[:, :384], right_panel[:384, at], preferred_element_type=F32)

    def incoming_second(n, at):
        part = total[:, at] + jnp.dot(
            left_panel[:, 384:896], right_panel[384:896, at], preferred_element_type=F32
        )
        for r in range(16):
            top = (r // 2) * LANES + (r % 2) * ROWS
            for k in range(WIDE // LANES):
                dest = r * 8 + n * (WIDE // LANES) + k
                slot = r * 2 + k
                folded(slot, 0, part[top : top + ROWS, k * LANES : (k + 1) * LANES])
                outs[8 + PA][dest] = flat_product[slot, 0:24].astype(BF16)
                outs[8 + PB][dest] = flat_product[slot, 24:48].astype(BF16)
                outs[8 + PX][dest] = flat_product[slot, 48:50].astype(BF16)

    rights, lefts = (8 + RA, 8 + RB), (8 + LA, 8 + LB)
    arrive(8 + RA)
    incoming_columns(0, 24, rights, False)
    arrive(8 + LA)
    incoming_columns(0, 24, lefts, True)
    wide(incoming_first)
    arrive(8 + RB, 8 + LB, 8 + LX)
    incoming_columns(24, 56, rights, False)
    incoming_columns(24, 56, lefts, True)
    wide(incoming_second)
    give(8 + PA)
    give(8 + PB, 8 + PX)
    arrive(8 + PA)
    mix(1, 0)
    for_tiles(0, FIRST, last)
    arrive(8 + PB, 8 + PX)
    mix(1, 1)
    for_tiles(FIRST, TILES, last)

    for number in range(16):
        others = outs[number].at[pl.ds(0, 127)]
        pltpu.make_async_copy(others, others, send_sem.at[number]).wait()


def body(pair_repr, *args):
    vmem, smem = (pl.BlockSpec(memory_space=m) for m in (pltpu.VMEM, pltpu.SMEM))
    messages = [pltpu.VMEM((CH, count, LANES), BF16) for count in MESSAGES]
    flat_shape = (TILES * LANES, CH)
    out = pl.pallas_call(
        kernel,
        out_shape=jax.ShapeDtypeStruct(flat_shape, BF16),
        in_specs=[pl.BlockSpec(memory_space=pl.ANY), smem, smem] + [vmem] * 7,
        out_specs=vmem,
        scratch_shapes=[
            pltpu.VMEM(flat_shape, BF16),
            pltpu.VMEM((TILES, CH, LANES), F32),
            pltpu.VMEM((TILES, CH, LANES), BF16),
            pltpu.VMEM((TILES, CH, LANES), F32),
            pltpu.VMEM((TILES * SKEW, LANES), F32),
            pltpu.VMEM((ROWS, LANES), F32),
            pltpu.VMEM((ROWS, LANES), F32),
            pltpu.VMEM((2, CH, LANES), F32),
            pltpu.VMEM((2, 4 * CH, CH), BF16),
            pltpu.VMEM((2, CH, CH), BF16),
            pltpu.VMEM((2, CH, CH), BF16),
            pltpu.VMEM((8 * LANES, 8 * LANES), BF16),
            pltpu.VMEM((8 * LANES, 8 * LANES), BF16),
            pltpu.VMEM((8 * LANES, 8 * LANES), F32),
            pltpu.VMEM((CH, 1, LANES), F32),
            pltpu.VMEM((CH, GROUP, LANES), F32),
            pltpu.VMEM((CH, 32, LANES), F32),
            pltpu.VMEM((16, 56, LANES), F32),
            pltpu.VMEM((32, 56, LANES), F32),
            *messages,
            *messages,
            pltpu.SemaphoreType.DMA((16,)),
            pltpu.SemaphoreType.DMA((16,)),
            pltpu.SemaphoreType.DMA((2,)),
        ],
        compiler_params=pltpu.CompilerParams(
            collective_id=0, has_side_effects=True, vmem_limit_bytes=62 << 20
        ),
    )(pair_repr.reshape(flat_shape), *args)
    return out.reshape(pair_repr.shape)


def solution(mesh):
    in_specs = (P("row", "col", None), P(), P(), P(), P(), P(), P(), P(), P(), P())
    out_specs = P("row", "col", None)
    return jax.shard_map(body, mesh=mesh, in_specs=in_specs, out_specs=out_specs, check_vma=False)
```

```python
import jax
import jax.numpy as jnp
from jax import lax
from jax.experimental import pallas as pl
from jax.experimental.pallas import tpu as pltpu
from jax.sharding import PartitionSpec as P

EPSILON = 1e-05
MESH = pl.DeviceIdType.MESH
F32 = jnp.float32
BF16 = jnp.bfloat16

ROWS = 56
COLS = 112
LANES = 128
TILES = 49
CH = 128
GROUP = 8
SHIFT = LANES - COLS
SKEW = 136
WIDE = 256
FIRST, SECOND = 24, 40
RA, RL, LB, LX, PA, PB, PX, QA, QB, QC, QX, QPA, QPB, QPC, QPX = range(15)
MESSAGES = (24, 56, 16, 2, 24, 24, 2) + (48, 32, 16, 2, 24, 16, 8, 2)


def peer(step, row, col):
    far = lax.rem(37 * step, 128)
    core = lax.rem(row + far, 2)
    x = lax.rem(row // 2 + far // 2, 4)
    z = lax.rem(col + far // 8, 4)
    y = lax.rem((col // 4) * 2 + row // 8 + far // 32, 4)
    return lax.rem(y, 2) * 8 + x * 2 + core, (y // 2) * 4 + z


def sigmoid(value):
    return 0.5 * jnp.tanh(0.5 * value) + 0.5


def for_each_peer(one):
    def turn(n, carry):
        for k in range(4):
            one(1 + n * 4 + k)
        return carry

    lax.fori_loop(0, 31, turn, 0)
    for step in range(125, 128):
        one(step)


def kernel(*refs):
    inputs, (out_hbm, *refs) = refs[:10], refs[10:]
    here, refs = refs[:10], refs[10:]
    x_ref, mask_ref, chain_ref, embed_ref, ab1_ref, gate1_ref, final1_ref, ab2_ref, gate2_ref, final2_ref = here
    out_ref, state, normed, gating, left_stage, right_stage, pair_mask, same_chain, embed_t, ab_t, gate_t, final_t, *refs = refs
    left_panel, right_panel, total, kept, products, flat, flat_product, *refs = refs
    LEFT, RIGHT = 0, 1
    stages = left_stage, right_stage
    count = len(MESSAGES)
    outs, ins = refs[:count], refs[count : 2 * count]
    send_sem, recv_sem, in_sem, out_sem = refs[2 * count :]
    row, col = lax.axis_index("row"), lax.axis_index("col")
    me = row * 8 + col
    barrier = pltpu.get_barrier_semaphore()

    copies = {}
    for name, k in (("mask", 1), ("chain", 2), ("embed", 3), ("ab1", 4)):
        copies[name] = pltpu.make_async_copy(inputs[k], here[k], in_sem.at[k])
        copies[name].start()
    x_copies, out_copies = [], []
    for number, (begin, end) in enumerate(((0, FIRST), (FIRST, TILES))):
        at = pl.ds(begin * LANES, (end - begin) * LANES)
        x_copies.append(pltpu.make_async_copy(inputs[0].at[at], x_ref.at[at], in_sem.at[10 * number]))
        x_copies[number].start()
    for number, (begin, end) in enumerate(((0, FIRST), (FIRST, SECOND), (SECOND, TILES))):
        at = pl.ds(begin * LANES, (end - begin) * LANES)
        out_copies.append(pltpu.make_async_copy(out_ref.at[at], out_hbm.at[at], out_sem.at[number]))

    def greet(row_to, col_to):
        pl.semaphore_signal(barrier, inc=1, device_id=(row_to, col_to), device_id_type=MESH)

    def greet_row(n, carry):
        for k in range(8):
            greet(lax.rem(row + n, 16), k)
        return carry

    for k in range(1, 8):
        greet(row, lax.rem(col + k, 8))
    lax.fori_loop(1, 16, greet_row, 0)
    for name, k in (("gate1", 5), ("final1", 6), ("ab2", 7), ("gate2", 8), ("final2", 9)):
        copies[name] = pltpu.make_async_copy(inputs[k], here[k], in_sem.at[k])
        copies[name].start()

    def turned(value):
        return value.astype(F32).T.astype(BF16)

    def turn_ab(update, ab, side):
        for part in (2 * side, 2 * side + 1):
            ab_t[update, part * CH : (part + 1) * CH, :] = turned(ab[:, part * CH : (part + 1) * CH])

    copies["mask"].wait()
    copies["chain"].wait()
    lane = lax.broadcasted_iota(jnp.int32, (1, LANES), 1)

    def collect(j, carry):
        mask, chain = carry
        here = lane == j
        mask = jnp.where(here, mask_ref[col * COLS + j], mask)
        return mask, jnp.where(here, chain_ref[col * COLS + j], chain)

    nothing = jnp.zeros((1, LANES), jnp.int32)
    col_mask, col_chain = lax.fori_loop(0, COLS, collect, (nothing, nothing), unroll=8)
    for phase in range(7):
        skip = SHIFT * phase

        def wrapped(value):
            value = value.astype(F32)
            near = pltpu.roll(value, LANES - skip, 1) if skip else value
            return jnp.where(lane < COLS - skip, near, pltpu.roll(value, COLS - skip, 1))

        tile_mask, tile_chain = wrapped(col_mask), wrapped(col_chain)
        for t in range(phase, TILES, 7):
            i = row * ROWS + t + t // 7
            near = lane < COLS - skip
            own_mask = jnp.where(near, mask_ref[i].astype(F32), mask_ref[i + 1].astype(F32))
            own_chain = jnp.where(near, chain_ref[i].astype(F32), chain_ref[i + 1].astype(F32))
            pair_mask[t : t + 1, :] = tile_mask * own_mask
            same_chain[t : t + 1, :] = jnp.where(tile_chain == own_chain, 1.0, 0.0)
    flat[...] = jnp.zeros(flat.shape, F32)

    lanes = lax.broadcasted_iota(jnp.int32, (GROUP, LANES), 1)
    row_of = lax.broadcasted_iota(jnp.int32, (GROUP, LANES), 0)
    from_former = lanes >= LANES - SHIFT * row_of
    from_same = lanes < COLS - SHIFT * row_of
    turn_back = (lanes + SHIFT * row_of) % LANES

    def unfold(tiles):
        mixed = jnp.where(from_former, pltpu.roll(tiles, 1, 0), tiles)
        return pltpu.roll(mixed, 0, 1, stride=SHIFT, stride_axis=0)

    def fold(rows):
        moved = jnp.take_along_axis(rows, turn_back, axis=1, mode="promise_in_bounds")
        return jnp.where(from_same, moved, pltpu.roll(moved, GROUP - 1, 0))

    def tile_at(t):
        return pl.ds(pl.multiple_of(t * SKEW, 8), CH)

    def positions(t):
        return pl.ds(pl.multiple_of(t * LANES, LANES), LANES)

    def start_state(t):
        same = jnp.broadcast_to(same_chain[pl.ds(t, 1), :], (CH, LANES)) > 0.5
        return x_ref[positions(t), :].astype(F32).T + jnp.where(same, embed_t[1], embed_t[0])

    def norm(value):
        center = value - jnp.sum(value, axis=0, keepdims=True) * (1.0 / CH)
        spread = jnp.sum(center * center, axis=0, keepdims=True) * (1.0 / CH)
        return (center * lax.rsqrt(spread + EPSILON)).astype(BF16)

    def operand(update, side, tiles, units):
        weights = ab_t[update, side * 2 * CH : (side + 1) * 2 * CH, :]
        both = jnp.dot(weights, jnp.concatenate(units, axis=1), preferred_element_type=F32)
        for k, t in enumerate(tiles):
            one = both[:, k * LANES : (k + 1) * LANES]
            stages[side][tile_at(t), :] = sigmoid(one[:CH]) * one[CH:] * pair_mask[pl.ds(t, 1), :]

    def for_tiles(begin, end, visit):
        def turn(n, carry):
            visit([begin + n * 4 + k for k in range(4)])
            return carry

        turns = (end - begin) // 4
        lax.fori_loop(0, turns, turn, 0)
        if begin + turns * 4 < end:
            visit(list(range(begin + turns * 4, end)))

    def send(number, row_to, col_to):
        pltpu.make_async_remote_copy(
            outs[number].at[row_to * 8 + col_to], ins[number].at[me],
            send_sem.at[number], recv_sem.at[number], device_id=(row_to, col_to), device_id_type=MESH,
        ).start()

    def staged(side, channel, begin, count):
        return stages[side][pl.ds(begin * SKEW + channel, count, stride=SKEW), :]

    def relay(make):
        def one(step):
            row_to, col_to = peer(step, row, col)
            channel = row_to * 8 + col_to
            for number, value in make(channel):
                outs[number][channel] = value.astype(BF16)
                send(number, row_to, col_to)

        for_each_peer(one)
        for number, value in make(me):
            ins[number][me] = value.astype(BF16)

    def arrive(*numbers):
        for number in numbers:
            others = ins[number].at[pl.ds(0, 127)]
            pltpu.make_async_copy(others, others, recv_sem.at[number]).wait()

    def give(*numbers):
        def one(step):
            row_to, col_to = peer(step, row, col)
            for number in numbers:
                send(number, row_to, col_to)

        for_each_peer(one)
        for number in numbers:
            ins[number][me] = outs[number][me]

    def got(number, source):
        return ins[number][source].astype(F32)

    def columns(visit):
        def turn(s, carry):
            visit(s, pl.ds(pl.multiple_of(s * LANES, LANES), LANES))
            return carry

        lax.fori_loop(0, 8, turn, 0)

    def wide(visit):
        def turn(n, carry):
            visit(n, pl.ds(pl.multiple_of(n * WIDE, WIDE), WIDE))
            return carry

        lax.fori_loop(0, 8 * LANES // WIDE, turn, 0)

    def unfolded(r, begin, end):
        return [unfold(flat[r, 7 * g : 7 * g + GROUP]) for g in range(begin, end)]

    def folded(slot, begin, rows):
        for g in range(rows.shape[0] // GROUP):
            at = 7 * (begin + g)
            flat_product[slot, at : at + GROUP] = fold(rows[g * GROUP : (g + 1) * GROUP])

    def mix(begin, count, tile_of):
        padded = -(-count // GROUP) * GROUP

        def add(c, carry):
            tile = tile_of(c)
            products[c, :padded] = tile
            return carry + tile

        empty = jnp.zeros((padded, LANES), F32)
        mean = lax.fori_loop(0, CH, add, empty, unroll=8) * (1.0 / CH)

        def add_square(c, carry):
            center = products[c, :padded] - mean
            return carry + center * center

        spread = lax.fori_loop(0, CH, add_square, empty, unroll=8) * (1.0 / CH)
        scale = lax.rsqrt(spread + EPSILON)

        def put(c, carry):
            value = (products[c, :padded] - mean) * scale
            left_stage[pl.ds(begin * SKEW + c, count, stride=SKEW), :] = value[:count]
            return carry

        lax.fori_loop(0, CH, put, 0, unroll=8)

    def got_with_row(number, extra, c):
        return jnp.concatenate([got(number, c), jnp.broadcast_to(got(extra, c)[0:1], (GROUP, LANES))], axis=0)

    def changed(update, tiles):
        mixed = jnp.concatenate([left_stage[tile_at(t), :].astype(BF16) for t in tiles], axis=1)
        change = jnp.dot(final_t[update], mixed, preferred_element_type=F32)
        return [
            state[t] + gating[t] * change[:, k * LANES : (k + 1) * LANES] for k, t in enumerate(tiles)
        ]

    def first(update, sides):
        def visit(tiles):
            values = [start_state(t) for t in tiles] if update == 0 else changed(0, tiles)
            units = [norm(value) for value in values]
            for t, value, unit in zip(tiles, values, units):
                state[t] = value
                normed[t] = unit
            for side in sides:
                operand(update, side, tiles, units)

        return visit

    def second(update):
        def visit(tiles):
            operand(update, LEFT, tiles, [normed[t] for t in tiles])

        return visit

    def third(update):
        def visit(tiles):
            units = jnp.concatenate([normed[t] for t in tiles], axis=1)
            gates = sigmoid(jnp.dot(gate_t[update], units, preferred_element_type=F32))
            for k, t in enumerate(tiles):
                gating[t] = gates[:, k * LANES : (k + 1) * LANES]

        return visit

    def last(tiles):
        for t, value in zip(tiles, changed(1, tiles)):
            out_ref[positions(t), :] = value.T.astype(BF16)

    copies["ab1"].wait()
    turn_ab(0, ab1_ref, RIGHT)
    copies["embed"].wait()
    for kind in range(2):
        embed_t[kind] = jnp.broadcast_to(embed_ref[kind : kind + 1, :], (CH, CH)).T
    x_copies[0].wait()
    for_tiles(0, FIRST, first(0, [RIGHT]))

    def right_early(channel):
        return [(RA, staged(RIGHT, channel, 0, FIRST))]

    def right_left(channel):
        tile = staged(LEFT, channel, 0, 32)
        last_right = jnp.broadcast_to(staged(RIGHT, channel, TILES - 1, 1), (GROUP, LANES))
        end = jnp.where(row_of == 7, last_right, tile[24:])
        return [(RL, jnp.concatenate([staged(RIGHT, channel, FIRST, 24), tile[:24], end], axis=0))]

    def left_late(channel):
        return [(LB, staged(LEFT, channel, 31, 16)), (LX, staged(LEFT, channel, 47, 2))]

    pl.semaphore_wait(barrier, 127)
    relay(right_early)
    turn_ab(0, ab1_ref, LEFT)
    x_copies[1].wait()
    for_tiles(FIRST, TILES, first(0, [RIGHT, LEFT]))
    for_tiles(0, FIRST, second(0))
    relay(right_left)
    relay(left_late)
    for name in ("gate1", "final1", "ab2", "gate2", "final2"):
        copies[name].wait()
    for update, (gate, final) in enumerate(((gate1_ref, final1_ref), (gate2_ref, final2_ref))):
        gate_t[update] = turned(gate[...])
        final_t[update] = turned(final[...])
    for side in (LEFT, RIGHT):
        turn_ab(1, ab2_ref, side)
    for_tiles(0, TILES, third(0))

    def right_columns(s, at):
        empty = jnp.zeros((LANES - 2 * ROWS, LANES), F32)
        for r in range(16):
            source = r * 8 + s
            both = got(RL, source)
            flat[r, 0:24] = got(RA, source)
            flat[r, 24:48] = both[:24]
            flat[r, 48:49] = both[55:]
        for a in range(8):
            rows = unfolded(2 * a, 0, 7) + unfolded(2 * a + 1, 0, 7)
            rows = [jnp.where(lanes < COLS, part, 0.0) for part in rows]
            right_panel[a * LANES : (a + 1) * LANES, at] = jnp.concatenate(rows + [empty], axis=0).astype(BF16)

    def left_columns_first(s, at):
        rows = []
        for r in range(16):
            flat[r, 0:32] = got(RL, r * 8 + s)[24:]
            rows += unfolded(r, 0, 4)
        left_panel[:512, at] = jnp.concatenate(rows, axis=0).astype(BF16)

    def left_columns_second(s, at):
        rows = []
        for r in range(16):
            source = r * 8 + s
            flat[r, 24:32] = got(RL, source)[48:]
            flat[r, 31:47] = got(LB, source)
            flat[r, 47:49] = got(LX, source)
            rows += unfolded(r, 4, 7)
        left_panel[512:896, at] = jnp.concatenate(rows, axis=0).astype(BF16)

    def outgoing_product(begin, end, half):
        count = (end - begin) // 16

        def visit(n, at):
            part = lax.dot_general(
                left_panel[begin:end, :], right_panel[at, :], (((1,), (1,)), ((), ())),
                preferred_element_type=F32,
            )
            for r in range(16):
                for k in range(WIDE // LANES):
                    block = part[r * count : (r + 1) * count, k * LANES : (k + 1) * LANES]
                    dest = r * 8 + n * (WIDE // LANES) + k
                    slot = r * 2 + k
                    if half == 0:
                        folded(slot, 0, block)
                        outs[PA][dest] = flat_product[slot, 0:24].astype(BF16)
                        kept[dest] = flat_product[slot, 24:32]
                    else:
                        flat_product[slot, 24:32] = kept[dest]
                        folded(slot, 4, block)
                        outs[PB][dest] = flat_product[slot, 24:48].astype(BF16)
                        outs[PX][dest] = flat_product[slot, 48:50].astype(BF16)

        wide(visit)

    arrive(RA, RL)
    columns(right_columns)
    columns(left_columns_first)
    outgoing_product(0, 512, 0)
    give(PA)
    arrive(LB, LX)
    columns(left_columns_second)
    outgoing_product(512, 896, 1)
    give(PB, PX)

    def both(number, begin, count):
        return lambda channel: [
            (number, jnp.concatenate([staged(side, channel, begin, count) for side in (RIGHT, LEFT)], axis=0))
        ]

    def rest(channel):
        extra = [staged(side, channel, TILES - 1, 1) for side in (RIGHT, LEFT)]
        return both(QC, SECOND, 8)(channel) + [(QX, jnp.concatenate(extra, axis=0))]

    arrive(PA)
    mix(0, 24, lambda c: got(PA, c))
    for_tiles(0, FIRST, first(1, [RIGHT, LEFT]))
    relay(both(QA, 0, FIRST))
    arrive(PB, PX)
    mix(24, 25, lambda c: got_with_row(PB, PX, c))
    for_tiles(FIRST, SECOND, first(1, [RIGHT, LEFT]))
    relay(both(QB, FIRST, 16))
    for_tiles(SECOND, TILES, first(1, [RIGHT, LEFT]))
    relay(rest)

    def incoming_columns(begin, end, numbers):
        depth = pl.ds(16 * begin, 16 * (end - begin))

        def visit(s, at):
            both_rows = [], []
            for r in range(16):
                source = r * 8 + s
                for k, side in enumerate((RIGHT, LEFT)):
                    slot = r + 16 * k
                    for top, number in numbers:
                        count = MESSAGES[number] // 2
                        if number == QX:
                            flat[slot, top : top + 1] = got(QX, source)[k : k + 1]
                        else:
                            flat[slot, top : top + count] = got(number, source)[k * count : (k + 1) * count]
                    both_rows[k].extend(unfolded(slot, begin // GROUP, end // GROUP))
            right_panel[depth, at] = jnp.concatenate(both_rows[0], axis=0).astype(BF16)
            left_panel[at, depth] = jnp.concatenate(both_rows[1], axis=0).T.astype(BF16)

        columns(visit)

    def incoming_part(begin, end, at):
        return jnp.dot(left_panel[:, begin:end], right_panel[begin:end, at], preferred_element_type=F32)

    def incoming_first(n, at):
        total[:, at] = incoming_part(0, 384, at)

    def incoming_second(n, at):
        total[:, at] += incoming_part(384, 640, at)

    def incoming_third(turn, carry):
        n = lax.rem(turn + row, 4)
        at = pl.ds(pl.multiple_of(n * WIDE, WIDE), WIDE)
        part = total[:, at] + incoming_part(640, 896, at)
        for r in range(16):
            top = (r // 2) * LANES + (r % 2) * ROWS
            for k in range(WIDE // LANES):
                dest = r * 8 + n * (WIDE // LANES) + k
                slot = r * 2 + k
                folded(slot, 0, part[top : top + ROWS, k * LANES : (k + 1) * LANES])
                outs[QPA][dest] = flat_product[slot, 0:24].astype(BF16)
                outs[QPB][dest] = flat_product[slot, 24:40].astype(BF16)
                outs[QPC][dest] = flat_product[slot, 40:48].astype(BF16)
                outs[QPX][dest] = flat_product[slot, 48:50].astype(BF16)
        for i in range(16):
            for k in range(WIDE // LANES):
                row_to = lax.rem(row + 5 * i, 16)
                col_to = n * (WIDE // LANES) + lax.rem(col + k, 2)
                if i == 0 and k == 0:
                    pl.when(row_to * 8 + col_to != me)(lambda: send(QPA, row_to, col_to))
                else:
                    send(QPA, row_to, col_to)
        return carry

    arrive(QA)
    incoming_columns(0, 24, [(0, QA)])
    wide(incoming_first)
    arrive(QB)
    incoming_columns(24, 40, [(0, QA), (24, QB)])
    wide(incoming_second)
    arrive(QC, QX)
    incoming_columns(40, 56, [(24, QB), (40, QC), (48, QX)])
    lax.fori_loop(0, 4, incoming_third, 0)
    ins[QPA][me] = outs[QPA][me]
    give(QPB)
    give(QPC, QPX)
    for_tiles(0, TILES, third(1))

    arrive(QPA)
    mix(0, 24, lambda c: got(QPA, c))
    for_tiles(0, FIRST, last)
    out_copies[0].start()
    arrive(QPB)
    mix(24, 16, lambda c: got(QPB, c))
    for_tiles(FIRST, SECOND, last)
    out_copies[1].start()
    arrive(QPC, QPX)
    mix(40, 9, lambda c: got_with_row(QPC, QPX, c))
    for_tiles(SECOND, TILES, last)
    out_copies[2].start()

    for number in range(len(MESSAGES)):
        others = outs[number].at[pl.ds(0, 127)]
        pltpu.make_async_copy(others, others, send_sem.at[number]).wait()
    for copy in out_copies:
        copy.wait()


def body(pair_repr, *args):
    messages = [pltpu.VMEM((CH, count, LANES), BF16) for count in MESSAGES]
    flat_shape = (TILES * LANES, CH)
    held = [pltpu.VMEM(flat_shape, BF16)]
    for number, arg in enumerate(args):
        held.append((pltpu.SMEM if number < 2 else pltpu.VMEM)(arg.shape, arg.dtype))
    out = pl.pallas_call(
        kernel,
        out_shape=pltpu.VMEM(flat_shape, BF16),
        in_specs=[pl.BlockSpec(memory_space=pltpu.HBM)] * 10,
        out_specs=pl.BlockSpec(memory_space=pl.ANY),
        scratch_shapes=[
            *held,
            pltpu.VMEM(flat_shape, BF16),
            pltpu.VMEM((TILES, CH, LANES), F32),
            pltpu.VMEM((TILES, CH, LANES), BF16),
            pltpu.VMEM((TILES, CH, LANES), F32),
            pltpu.VMEM((TILES * SKEW, LANES), F32),
            pltpu.VMEM((TILES * SKEW, LANES), F32),
            pltpu.VMEM((ROWS, LANES), F32),
            pltpu.VMEM((ROWS, LANES), F32),
            pltpu.VMEM((2, CH, LANES), F32),
            pltpu.VMEM((2, 4 * CH, CH), BF16),
            pltpu.VMEM((2, CH, CH), BF16),
            pltpu.VMEM((2, CH, CH), BF16),
            pltpu.VMEM((8 * LANES, 8 * LANES), BF16),
            pltpu.VMEM((8 * LANES, 8 * LANES), BF16),
            pltpu.VMEM((8 * LANES, 8 * LANES), F32),
            pltpu.VMEM((CH, GROUP, LANES), F32),
            pltpu.VMEM((CH, 32, LANES), F32),
            pltpu.VMEM((32, 56, LANES), F32),
            pltpu.VMEM((32, 56, LANES), F32),
            *messages,
            *messages,
            pltpu.SemaphoreType.DMA((len(MESSAGES),)),
            pltpu.SemaphoreType.DMA((len(MESSAGES),)),
            pltpu.SemaphoreType.DMA((11,)),
            pltpu.SemaphoreType.DMA((3,)),
        ],
        compiler_params=pltpu.CompilerParams(
            collective_id=0, has_side_effects=True, vmem_limit_bytes=56 << 20
        ),
    )(*(pltpu.with_memory_space_constraint(a, pltpu.HBM) for a in (pair_repr.reshape(flat_shape), *args)))
    return out.reshape(pair_repr.shape)


def solution(mesh):
    in_specs = (P("row", "col", None), P(), P(), P(), P(), P(), P(), P(), P(), P())
    out_specs = P("row", "col", None)
    return jax.shard_map(body, mesh=mesh, in_specs=in_specs, out_specs=out_specs, check_vma=False)
```

```python
import jax
import jax.numpy as jnp
from jax import lax
from jax.experimental import pallas as pl
from jax.experimental.pallas import tpu as pltpu
from jax.sharding import PartitionSpec as P

EPSILON = 1e-05
MESH = pl.DeviceIdType.MESH
F32 = jnp.float32
BF16 = jnp.bfloat16

ROWS = 56
COLS = 112
LANES = 128
TILES = 49
CH = 128
GROUP = 8
SHIFT = LANES - COLS
SKEW = 136
WIDE = 256
FIRST, SECOND = 24, 40
RA, RB, LA, LB, LX, PA, PB, PX, QA, QB, QC, QX, QPA, QPB, QPC, QPX = range(16)
MESSAGES = (24, 24, 32, 16, 2, 24, 24, 2) + (48, 32, 16, 2, 24, 16, 8, 2)


def peer(step, row, col):
    far = lax.rem(37 * step, 128)
    core = lax.rem(row + far, 2)
    x = lax.rem(row // 2 + far // 2, 4)
    z = lax.rem(col + far // 8, 4)
    y = lax.rem((col // 4) * 2 + row // 8 + far // 32, 4)
    return lax.rem(y, 2) * 8 + x * 2 + core, (y // 2) * 4 + z


def sigmoid(value):
    return 0.5 * jnp.tanh(0.5 * value) + 0.5


def for_each_peer(one):
    def turn(n, carry):
        for k in range(4):
            one(1 + n * 4 + k)
        return carry

    lax.fori_loop(0, 31, turn, 0)
    for step in range(125, 128):
        one(step)


def kernel(*refs):
    inputs, (out_hbm, *refs) = refs[:10], refs[10:]
    here, refs = refs[:10], refs[10:]
    x_ref, mask_ref, chain_ref, embed_ref, ab1_ref, gate1_ref, final1_ref, ab2_ref, gate2_ref, final2_ref = here
    out_ref, state, normed, gating, left_stage, right_stage, pair_mask, same_chain, embed_t, ab_t, gate_t, final_t, *refs = refs
    left_panel, right_panel, total, kept, products, flat, flat_product, *refs = refs
    LEFT, RIGHT = 0, 1
    stages = left_stage, right_stage
    count = len(MESSAGES)
    outs, ins = refs[:count], refs[count : 2 * count]
    send_sem, recv_sem, in_sem, out_sem = refs[2 * count :]
    row, col = lax.axis_index("row"), lax.axis_index("col")
    me = row * 8 + col
    barrier = pltpu.get_barrier_semaphore()

    copies = {}
    for name, k in (("mask", 1), ("chain", 2), ("embed", 3), ("ab1", 4)):
        copies[name] = pltpu.make_async_copy(inputs[k], here[k], in_sem.at[k])
        copies[name].start()
    x_copies, out_copies = [], []
    for number, (begin, end) in enumerate(((0, FIRST), (FIRST, TILES))):
        at = pl.ds(begin * LANES, (end - begin) * LANES)
        x_copies.append(pltpu.make_async_copy(inputs[0].at[at], x_ref.at[at], in_sem.at[10 * number]))
        x_copies[number].start()
    for number, (begin, end) in enumerate(((0, FIRST), (FIRST, SECOND), (SECOND, TILES))):
        at = pl.ds(begin * LANES, (end - begin) * LANES)
        out_copies.append(pltpu.make_async_copy(out_ref.at[at], out_hbm.at[at], out_sem.at[number]))

    def greet(row_to, col_to):
        pl.semaphore_signal(barrier, inc=1, device_id=(row_to, col_to), device_id_type=MESH)

    def greet_row(n, carry):
        for k in range(8):
            greet(lax.rem(row + n, 16), k)
        return carry

    for k in range(1, 8):
        greet(row, lax.rem(col + k, 8))
    lax.fori_loop(1, 16, greet_row, 0)
    for name, k in (("gate1", 5), ("final1", 6), ("ab2", 7), ("gate2", 8), ("final2", 9)):
        copies[name] = pltpu.make_async_copy(inputs[k], here[k], in_sem.at[k])
        copies[name].start()

    def turned(value):
        return value.astype(F32).T.astype(BF16)

    def turn_ab(update, ab, side):
        for part in (2 * side, 2 * side + 1):
            ab_t[update, part * CH : (part + 1) * CH, :] = turned(ab[:, part * CH : (part + 1) * CH])

    copies["mask"].wait()
    copies["chain"].wait()
    lane = lax.broadcasted_iota(jnp.int32, (1, LANES), 1)

    def collect(j, carry):
        mask, chain = carry
        here = lane == j
        mask = jnp.where(here, mask_ref[col * COLS + j], mask)
        return mask, jnp.where(here, chain_ref[col * COLS + j], chain)

    nothing = jnp.zeros((1, LANES), jnp.int32)
    col_mask, col_chain = lax.fori_loop(0, COLS, collect, (nothing, nothing), unroll=8)
    for phase in range(7):
        skip = SHIFT * phase

        def wrapped(value):
            value = value.astype(F32)
            near = pltpu.roll(value, LANES - skip, 1) if skip else value
            return jnp.where(lane < COLS - skip, near, pltpu.roll(value, COLS - skip, 1))

        tile_mask, tile_chain = wrapped(col_mask), wrapped(col_chain)
        for t in range(phase, TILES, 7):
            i = row * ROWS + t + t // 7
            near = lane < COLS - skip
            own_mask = jnp.where(near, mask_ref[i].astype(F32), mask_ref[i + 1].astype(F32))
            own_chain = jnp.where(near, chain_ref[i].astype(F32), chain_ref[i + 1].astype(F32))
            pair_mask[t : t + 1, :] = tile_mask * own_mask
            same_chain[t : t + 1, :] = jnp.where(tile_chain == own_chain, 1.0, 0.0)
    flat[...] = jnp.zeros(flat.shape, F32)

    lanes = lax.broadcasted_iota(jnp.int32, (GROUP, LANES), 1)
    row_of = lax.broadcasted_iota(jnp.int32, (GROUP, LANES), 0)
    from_former = lanes >= LANES - SHIFT * row_of
    from_same = lanes < COLS - SHIFT * row_of
    turn_back = (lanes + SHIFT * row_of) % LANES

    def unfold(tiles):
        mixed = jnp.where(from_former, pltpu.roll(tiles, 1, 0), tiles)
        return pltpu.roll(mixed, 0, 1, stride=SHIFT, stride_axis=0)

    def fold(rows):
        moved = jnp.take_along_axis(rows, turn_back, axis=1, mode="promise_in_bounds")
        return jnp.where(from_same, moved, pltpu.roll(moved, GROUP - 1, 0))

    def tile_at(t):
        return pl.ds(pl.multiple_of(t * SKEW, 8), CH)

    def positions(t):
        return pl.ds(pl.multiple_of(t * LANES, LANES), LANES)

    def start_state(t):
        same = jnp.broadcast_to(same_chain[pl.ds(t, 1), :], (CH, LANES)) > 0.5
        return x_ref[positions(t), :].astype(F32).T + jnp.where(same, embed_t[1], embed_t[0])

    def norm(value):
        center = value - jnp.sum(value, axis=0, keepdims=True) * (1.0 / CH)
        spread = jnp.sum(center * center, axis=0, keepdims=True) * (1.0 / CH)
        return (center * lax.rsqrt(spread + EPSILON)).astype(BF16)

    def operand(update, side, tiles, units):
        weights = ab_t[update, side * 2 * CH : (side + 1) * 2 * CH, :]
        both = jnp.dot(weights, jnp.concatenate(units, axis=1), preferred_element_type=F32)
        for k, t in enumerate(tiles):
            one = both[:, k * LANES : (k + 1) * LANES]
            stages[side][tile_at(t), :] = sigmoid(one[:CH]) * one[CH:] * pair_mask[pl.ds(t, 1), :]

    def for_tiles(begin, end, visit):
        def turn(n, carry):
            visit([begin + n * 4 + k for k in range(4)])
            return carry

        turns = (end - begin) // 4
        lax.fori_loop(0, turns, turn, 0)
        if begin + turns * 4 < end:
            visit(list(range(begin + turns * 4, end)))

    def send(number, row_to, col_to):
        pltpu.make_async_remote_copy(
            outs[number].at[row_to * 8 + col_to], ins[number].at[me],
            send_sem.at[number], recv_sem.at[number], device_id=(row_to, col_to), device_id_type=MESH,
        ).start()

    def staged(side, channel, begin, count):
        return stages[side][pl.ds(begin * SKEW + channel, count, stride=SKEW), :]

    def relay(make):
        def one(step):
            row_to, col_to = peer(step, row, col)
            channel = row_to * 8 + col_to
            for number, value in make(channel):
                outs[number][channel] = value.astype(BF16)
                send(number, row_to, col_to)

        for_each_peer(one)
        for number, value in make(me):
            ins[number][me] = value.astype(BF16)

    def arrive(*numbers):
        for number in numbers:
            others = ins[number].at[pl.ds(0, 127)]
            pltpu.make_async_copy(others, others, recv_sem.at[number]).wait()

    def give(*numbers):
        def one(step):
            row_to, col_to = peer(step, row, col)
            for number in numbers:
                send(number, row_to, col_to)

        for_each_peer(one)
        for number in numbers:
            ins[number][me] = outs[number][me]

    def got(number, source):
        return ins[number][source].astype(F32)

    def columns(visit):
        def turn(s, carry):
            visit(s, pl.ds(pl.multiple_of(s * LANES, LANES), LANES))
            return carry

        lax.fori_loop(0, 8, turn, 0)

    def wide(visit):
        def turn(n, carry):
            visit(n, pl.ds(pl.multiple_of(n * WIDE, WIDE), WIDE))
            return carry

        lax.fori_loop(0, 8 * LANES // WIDE, turn, 0)

    def wide_and_send(visit, number):
        def turn(n, carry):
            n = lax.rem(n + row, 8 * LANES // WIDE)
            visit(n, pl.ds(pl.multiple_of(n * WIDE, WIDE), WIDE))
            for i in range(16):
                for k in range(WIDE // LANES):
                    row_to = lax.rem(row + 5 * i, 16)
                    col_to = n * (WIDE // LANES) + lax.rem(col + k, 2)
                    if i == 0 and k == 0:
                        pl.when(row_to * 8 + col_to != me)(lambda: send(number, row_to, col_to))
                    else:
                        send(number, row_to, col_to)
            return carry

        lax.fori_loop(0, 8 * LANES // WIDE, turn, 0)
        ins[number][me] = outs[number][me]

    def unfolded(r, begin, end):
        return [unfold(flat[r, 7 * g : 7 * g + GROUP]) for g in range(begin, end)]

    def folded(slot, begin, rows):
        for g in range(rows.shape[0] // GROUP):
            at = 7 * (begin + g)
            flat_product[slot, at : at + GROUP] = fold(rows[g * GROUP : (g + 1) * GROUP])

    def mix(begin, count, tile_of):
        padded = -(-count // GROUP) * GROUP

        def add(c, carry):
            tile = tile_of(c)
            products[c, :padded] = tile
            return carry + tile

        empty = jnp.zeros((padded, LANES), F32)
        mean = lax.fori_loop(0, CH, add, empty, unroll=8) * (1.0 / CH)

        def add_square(c, carry):
            center = products[c, :padded] - mean
            return carry + center * center

        spread = lax.fori_loop(0, CH, add_square, empty, unroll=8) * (1.0 / CH)
        scale = lax.rsqrt(spread + EPSILON)

        def put(c, carry):
            value = (products[c, :padded] - mean) * scale
            left_stage[pl.ds(begin * SKEW + c, count, stride=SKEW), :] = value[:count]
            return carry

        lax.fori_loop(0, CH, put, 0, unroll=8)

    def got_with_row(number, extra, c):
        return jnp.concatenate([got(number, c), jnp.broadcast_to(got(extra, c)[0:1], (GROUP, LANES))], axis=0)

    def changed(update, tiles):
        mixed = jnp.concatenate([left_stage[tile_at(t), :].astype(BF16) for t in tiles], axis=1)
        change = jnp.dot(final_t[update], mixed, preferred_element_type=F32)
        return [
            state[t] + gating[t] * change[:, k * LANES : (k + 1) * LANES] for k, t in enumerate(tiles)
        ]

    def first(update, sides):
        def visit(tiles):
            values = [start_state(t) for t in tiles] if update == 0 else changed(0, tiles)
            units = [norm(value) for value in values]
            for t, value, unit in zip(tiles, values, units):
                state[t] = value
                normed[t] = unit
            for side in sides:
                operand(update, side, tiles, units)

        return visit

    def second(update):
        def visit(tiles):
            operand(update, LEFT, tiles, [normed[t] for t in tiles])

        return visit

    def third(update):
        def visit(tiles):
            units = jnp.concatenate([normed[t] for t in tiles], axis=1)
            gates = sigmoid(jnp.dot(gate_t[update], units, preferred_element_type=F32))
            for k, t in enumerate(tiles):
                gating[t] = gates[:, k * LANES : (k + 1) * LANES]

        return visit

    def last(tiles):
        for t, value in zip(tiles, changed(1, tiles)):
            out_ref[positions(t), :] = value.T.astype(BF16)

    copies["ab1"].wait()
    turn_ab(0, ab1_ref, RIGHT)
    copies["embed"].wait()
    for kind in range(2):
        embed_t[kind] = jnp.broadcast_to(embed_ref[kind : kind + 1, :], (CH, CH)).T
    x_copies[0].wait()
    for_tiles(0, FIRST, first(0, [RIGHT]))

    def right_early(channel):
        return [(RA, staged(RIGHT, channel, 0, FIRST))]

    def right_late(channel):
        return [(RB, staged(RIGHT, channel, FIRST, 24))]

    def left_early(channel):
        tile = staged(LEFT, channel, 0, 32)
        last_right = jnp.broadcast_to(staged(RIGHT, channel, TILES - 1, 1), (GROUP, LANES))
        end = jnp.where(row_of == 7, last_right, tile[24:])
        return [(LA, jnp.concatenate([tile[:24], end], axis=0))]

    def left_late(channel):
        return [(LB, staged(LEFT, channel, 31, 16)), (LX, staged(LEFT, channel, 47, 2))]

    pl.semaphore_wait(barrier, 127)
    relay(right_early)
    x_copies[1].wait()
    for_tiles(FIRST, TILES, first(0, [RIGHT]))
    relay(right_late)
    turn_ab(0, ab1_ref, LEFT)
    for_tiles(0, TILES, second(0))
    relay(left_early)
    relay(left_late)
    for name in ("gate1", "final1", "ab2", "gate2", "final2"):
        copies[name].wait()
    for update, (gate, final) in enumerate(((gate1_ref, final1_ref), (gate2_ref, final2_ref))):
        gate_t[update] = turned(gate[...])
        final_t[update] = turned(final[...])
    for side in (LEFT, RIGHT):
        turn_ab(1, ab2_ref, side)
    for_tiles(0, TILES, third(0))

    def right_columns_most(s, at):
        for r in range(16):
            source = r * 8 + s
            flat[r, 0:24] = got(RA, source)
            flat[r, 24:48] = got(RB, source)
            rows = [jnp.where(lanes < COLS, part, 0.0) for part in unfolded(r, 0, 6)]
            top = (r // 2) * LANES + (r % 2) * ROWS
            total[top : top + 48, at] = jnp.concatenate(rows, axis=0)

    def right_columns(s, at):
        rows = []
        for r in range(16):
            source = r * 8 + s
            flat[r, 40:48] = got(RB, source)[16:]
            flat[r, 48:49] = got(LA, source)[31:]
            top = (r // 2) * LANES + (r % 2) * ROWS
            rows += [total[top : top + 48, at], jnp.where(lanes < COLS, unfolded(r, 6, 7)[0], 0.0)]
        empty = jnp.zeros((LANES - 2 * ROWS, LANES), F32)
        for a in range(8):
            panel = jnp.concatenate(rows[4 * a : 4 * a + 4] + [empty], axis=0)
            right_panel[a * LANES : (a + 1) * LANES, at] = panel.astype(BF16)

    def left_columns_first(s, at):
        rows = []
        for r in range(16):
            flat[r, 0:32] = got(LA, r * 8 + s)
            rows += unfolded(r, 0, 4)
        left_panel[:512, at] = jnp.concatenate(rows, axis=0).astype(BF16)

    def left_columns_second(s, at):
        rows = []
        for r in range(16):
            source = r * 8 + s
            flat[r, 24:32] = got(LA, source)[24:]
            flat[r, 31:47] = got(LB, source)
            flat[r, 47:49] = got(LX, source)
            rows += unfolded(r, 4, 7)
        left_panel[512:896, at] = jnp.concatenate(rows, axis=0).astype(BF16)

    def outgoing_product(begin, end, half):
        count = (end - begin) // 16

        def visit(n, at):
            part = lax.dot_general(
                left_panel[begin:end, :], right_panel[at, :], (((1,), (1,)), ((), ())),
                preferred_element_type=F32,
            )
            for r in range(16):
                for k in range(WIDE // LANES):
                    block = part[r * count : (r + 1) * count, k * LANES : (k + 1) * LANES]
                    dest = r * 8 + n * (WIDE // LANES) + k
                    slot = r * 2 + k
                    if half == 0:
                        folded(slot, 0, block)
                        outs[PA][dest] = flat_product[slot, 0:24].astype(BF16)
                        kept[dest] = flat_product[slot, 24:32]
                    else:
                        flat_product[slot, 24:32] = kept[dest]
                        folded(slot, 4, block)
                        outs[PB][dest] = flat_product[slot, 24:48].astype(BF16)
                        outs[PX][dest] = flat_product[slot, 48:50].astype(BF16)

        if half == 0:
            wide_and_send(visit, PA)
        else:
            wide(visit)

    arrive(RA, RB)
    columns(right_columns_most)
    arrive(LA)
    columns(right_columns)
    columns(left_columns_first)
    outgoing_product(0, 512, 0)
    arrive(LB, LX)
    columns(left_columns_second)
    outgoing_product(512, 896, 1)
    give(PB, PX)

    def both(number, begin, count):
        return lambda channel: [
            (number, jnp.concatenate([staged(side, channel, begin, count) for side in (RIGHT, LEFT)], axis=0))
        ]

    def rest(channel):
        extra = [staged(side, channel, TILES - 1, 1) for side in (RIGHT, LEFT)]
        return both(QC, SECOND, 8)(channel) + [(QX, jnp.concatenate(extra, axis=0))]

    arrive(PA)
    mix(0, 24, lambda c: got(PA, c))
    for_tiles(0, FIRST, first(1, [RIGHT, LEFT]))
    relay(both(QA, 0, FIRST))
    arrive(PB, PX)
    mix(24, 25, lambda c: got_with_row(PB, PX, c))
    for_tiles(FIRST, SECOND, first(1, [RIGHT, LEFT]))
    relay(both(QB, FIRST, 16))
    for_tiles(SECOND, TILES, first(1, [RIGHT, LEFT]))
    relay(rest)

    def incoming_columns(begin, end, numbers):
        depth = pl.ds(16 * begin, 16 * (end - begin))

        def visit(s, at):
            both_rows = [], []
            for r in range(16):
                source = r * 8 + s
                for k, side in enumerate((RIGHT, LEFT)):
                    slot = r + 16 * k
                    for top, number in numbers:
                        count = MESSAGES[number] // 2
                        if number == QX:
                            flat[slot, top : top + 1] = got(QX, source)[k : k + 1]
                        else:
                            flat[slot, top : top + count] = got(number, source)[k * count : (k + 1) * count]
                    both_rows[k].extend(unfolded(slot, begin // GROUP, end // GROUP))
            right_panel[depth, at] = jnp.concatenate(both_rows[0], axis=0).astype(BF16)
            left_panel[at, depth] = jnp.concatenate(both_rows[1], axis=0).T.astype(BF16)

        columns(visit)

    def incoming_part(begin, end, at):
        return jnp.dot(left_panel[:, begin:end], right_panel[begin:end, at], preferred_element_type=F32)

    def incoming_first(n, at):
        total[:, at] = incoming_part(0, 384, at)

    def incoming_second(n, at):
        total[:, at] += incoming_part(384, 640, at)

    def incoming_third(n, at):
        part = total[:, at] + incoming_part(640, 896, at)
        for r in range(16):
            top = (r // 2) * LANES + (r % 2) * ROWS
            for k in range(WIDE // LANES):
                dest = r * 8 + n * (WIDE // LANES) + k
                slot = r * 2 + k
                folded(slot, 0, part[top : top + ROWS, k * LANES : (k + 1) * LANES])
                outs[QPA][dest] = flat_product[slot, 0:24].astype(BF16)
                outs[QPB][dest] = flat_product[slot, 24:40].astype(BF16)
                outs[QPC][dest] = flat_product[slot, 40:48].astype(BF16)
                outs[QPX][dest] = flat_product[slot, 48:50].astype(BF16)

    arrive(QA)
    incoming_columns(0, 24, [(0, QA)])
    wide(incoming_first)
    arrive(QB)
    incoming_columns(24, 40, [(0, QA), (24, QB)])
    wide(incoming_second)
    arrive(QC, QX)
    incoming_columns(40, 56, [(24, QB), (40, QC), (48, QX)])
    wide_and_send(incoming_third, QPA)
    give(QPB)
    give(QPC, QPX)
    for_tiles(0, TILES, third(1))

    arrive(QPA)
    mix(0, 24, lambda c: got(QPA, c))
    for_tiles(0, FIRST, last)
    out_copies[0].start()
    arrive(QPB)
    mix(24, 16, lambda c: got(QPB, c))
    for_tiles(FIRST, SECOND, last)
    out_copies[1].start()
    arrive(QPC, QPX)
    mix(40, 9, lambda c: got_with_row(QPC, QPX, c))
    for_tiles(SECOND, TILES, last)
    out_copies[2].start()

    for number in range(len(MESSAGES)):
        others = outs[number].at[pl.ds(0, 127)]
        pltpu.make_async_copy(others, others, send_sem.at[number]).wait()
    for copy in out_copies:
        copy.wait()


def body(pair_repr, *args):
    messages = [pltpu.VMEM((CH, count, LANES), BF16) for count in MESSAGES]
    flat_shape = (TILES * LANES, CH)
    held = [pltpu.VMEM(flat_shape, BF16)]
    for number, arg in enumerate(args):
        held.append((pltpu.SMEM if number < 2 else pltpu.VMEM)(arg.shape, arg.dtype))
    out = pl.pallas_call(
        kernel,
        out_shape=pltpu.VMEM(flat_shape, BF16),
        in_specs=[pl.BlockSpec(memory_space=pltpu.HBM)] * 10,
        out_specs=pl.BlockSpec(memory_space=pl.ANY),
        scratch_shapes=[
            *held,
            pltpu.VMEM(flat_shape, BF16),
            pltpu.VMEM((TILES, CH, LANES), F32),
            pltpu.VMEM((TILES, CH, LANES), BF16),
            pltpu.VMEM((TILES, CH, LANES), F32),
            pltpu.VMEM((TILES * SKEW, LANES), F32),
            pltpu.VMEM((TILES * SKEW, LANES), F32),
            pltpu.VMEM((ROWS, LANES), F32),
            pltpu.VMEM((ROWS, LANES), F32),
            pltpu.VMEM((2, CH, LANES), F32),
            pltpu.VMEM((2, 4 * CH, CH), BF16),
            pltpu.VMEM((2, CH, CH), BF16),
            pltpu.VMEM((2, CH, CH), BF16),
            pltpu.VMEM((8 * LANES, 8 * LANES), BF16),
            pltpu.VMEM((8 * LANES, 8 * LANES), BF16),
            pltpu.VMEM((8 * LANES, 8 * LANES), F32),
            pltpu.VMEM((CH, GROUP, LANES), F32),
            pltpu.VMEM((CH, 32, LANES), F32),
            pltpu.VMEM((32, 56, LANES), F32),
            pltpu.VMEM((32, 56, LANES), F32),
            *messages,
            *messages,
            pltpu.SemaphoreType.DMA((len(MESSAGES),)),
            pltpu.SemaphoreType.DMA((len(MESSAGES),)),
            pltpu.SemaphoreType.DMA((11,)),
            pltpu.SemaphoreType.DMA((3,)),
        ],
        compiler_params=pltpu.CompilerParams(
            collective_id=0, has_side_effects=True, vmem_limit_bytes=56 << 20
        ),
    )(*(pltpu.with_memory_space_constraint(a, pltpu.HBM) for a in (pair_repr.reshape(flat_shape), *args)))
    return out.reshape(pair_repr.shape)


def solution(mesh):
    in_specs = (P("row", "col", None), P(), P(), P(), P(), P(), P(), P(), P(), P())
    out_specs = P("row", "col", None)
    return jax.shard_map(body, mesh=mesh, in_specs=in_specs, out_specs=out_specs, check_vma=False)
```

```python
import jax
import jax.numpy as jnp
from jax import lax
from jax.experimental import pallas as pl
from jax.experimental.pallas import tpu as pltpu
from jax.sharding import PartitionSpec as P

EPSILON = 1e-05
MESH = pl.DeviceIdType.MESH
F32 = jnp.float32
BF16 = jnp.bfloat16

ROWS = 56
COLS = 112
LANES = 128
TILES = 49
CH = 128
GROUP = 8
SHIFT = LANES - COLS
SKEW = 136
WIDE = 256
FIRST, SECOND = 24, 40
RA, RB, LA, LB, LX, PA, PB, PX, QRA, QLA, QB, QC, QX, QPA, QPB, QPC, QPX = range(17)
MESSAGES = (24, 24, 32, 16, 2, 24, 24, 2) + (24, 24, 32, 16, 2, 24, 16, 8, 2)


def peer(step, row, col):
    far = lax.rem(59 * step, 128)
    core = lax.rem(row + far, 2)
    x = lax.rem(row // 2 + far // 2, 4)
    z = lax.rem(col + far // 8, 4)
    y = lax.rem((col // 4) * 2 + row // 8 + far // 32, 4)
    return lax.rem(y, 2) * 8 + x * 2 + core, (y // 2) * 4 + z


def sigmoid(value):
    return 0.5 * jnp.tanh(0.5 * value) + 0.5


def for_each_peer(one):
    def turn(n, carry):
        for k in range(4):
            one(1 + n * 4 + k)
        return carry

    lax.fori_loop(0, 31, turn, 0)
    for step in range(125, 128):
        one(step)


def kernel(*refs):
    inputs, (out_hbm, *refs) = refs[:10], refs[10:]
    here, refs = refs[:10], refs[10:]
    x_ref, mask_ref, chain_ref, embed_ref, ab1_ref, gate1_ref, final1_ref, ab2_ref, gate2_ref, final2_ref = here
    out_ref, state, normed, gating, left_stage, right_stage, pair_mask, same_chain, embed_t, ab_t, gate_t, final_t, *refs = refs
    left_panel, right_panel, total, kept, products, flat, flat_product, *refs = refs
    LEFT, RIGHT = 0, 1
    stages = left_stage, right_stage
    count = len(MESSAGES)
    outs, ins = refs[:count], refs[count : 2 * count]
    send_sem, recv_sem, in_sem, out_sem = refs[2 * count :]
    row, col = lax.axis_index("row"), lax.axis_index("col")
    me = row * 8 + col
    barrier = pltpu.get_barrier_semaphore()

    copies = {}
    for name, k in (("mask", 1), ("chain", 2), ("embed", 3), ("ab1", 4)):
        copies[name] = pltpu.make_async_copy(inputs[k], here[k], in_sem.at[k])
        copies[name].start()
    x_copies, out_copies = [], []
    for number, (begin, end) in enumerate(((0, FIRST), (FIRST, TILES))):
        at = pl.ds(begin * LANES, (end - begin) * LANES)
        x_copies.append(pltpu.make_async_copy(inputs[0].at[at], x_ref.at[at], in_sem.at[10 * number]))
        x_copies[number].start()
    for number, (begin, end) in enumerate(((0, FIRST), (FIRST, SECOND), (SECOND, TILES))):
        at = pl.ds(begin * LANES, (end - begin) * LANES)
        out_copies.append(pltpu.make_async_copy(out_ref.at[at], out_hbm.at[at], out_sem.at[number]))

    def greet(row_to, col_to):
        pl.semaphore_signal(barrier, inc=1, device_id=(row_to, col_to), device_id_type=MESH)

    def greet_row(n, carry):
        for k in range(8):
            greet(lax.rem(row + n, 16), k)
        return carry

    for k in range(1, 8):
        greet(row, lax.rem(col + k, 8))
    lax.fori_loop(1, 16, greet_row, 0)
    for name, k in (("gate1", 5), ("final1", 6), ("ab2", 7), ("gate2", 8), ("final2", 9)):
        copies[name] = pltpu.make_async_copy(inputs[k], here[k], in_sem.at[k])
        copies[name].start()

    def turned(value):
        return value.astype(F32).T.astype(BF16)

    def turn_ab(update, ab, side):
        for part in (2 * side, 2 * side + 1):
            ab_t[update, part * CH : (part + 1) * CH, :] = turned(ab[:, part * CH : (part + 1) * CH])

    copies["mask"].wait()
    copies["chain"].wait()
    lane = lax.broadcasted_iota(jnp.int32, (1, LANES), 1)

    def collect(j, carry):
        mask, chain = carry
        here = lane == j
        mask = jnp.where(here, mask_ref[col * COLS + j], mask)
        return mask, jnp.where(here, chain_ref[col * COLS + j], chain)

    nothing = jnp.zeros((1, LANES), jnp.int32)
    col_mask, col_chain = lax.fori_loop(0, COLS, collect, (nothing, nothing), unroll=8)
    for phase in range(7):
        skip = SHIFT * phase

        def wrapped(value):
            value = value.astype(F32)
            near = pltpu.roll(value, LANES - skip, 1) if skip else value
            return jnp.where(lane < COLS - skip, near, pltpu.roll(value, COLS - skip, 1))

        tile_mask, tile_chain = wrapped(col_mask), wrapped(col_chain)
        for t in range(phase, TILES, 7):
            i = row * ROWS + t + t // 7
            near = lane < COLS - skip
            own_mask = jnp.where(near, mask_ref[i].astype(F32), mask_ref[i + 1].astype(F32))
            own_chain = jnp.where(near, chain_ref[i].astype(F32), chain_ref[i + 1].astype(F32))
            pair_mask[t : t + 1, :] = tile_mask * own_mask
            same_chain[t : t + 1, :] = jnp.where(tile_chain == own_chain, 1.0, 0.0)
    flat[...] = jnp.zeros(flat.shape, F32)

    lanes = lax.broadcasted_iota(jnp.int32, (GROUP, LANES), 1)
    row_of = lax.broadcasted_iota(jnp.int32, (GROUP, LANES), 0)
    from_former = lanes >= LANES - SHIFT * row_of
    from_same = lanes < COLS - SHIFT * row_of
    turn_back = (lanes + SHIFT * row_of) % LANES

    def unfold(tiles):
        mixed = jnp.where(from_former, pltpu.roll(tiles, 1, 0), tiles)
        return pltpu.roll(mixed, 0, 1, stride=SHIFT, stride_axis=0)

    def fold(rows):
        moved = jnp.take_along_axis(rows, turn_back, axis=1, mode="promise_in_bounds")
        return jnp.where(from_same, moved, pltpu.roll(moved, GROUP - 1, 0))

    def tile_at(t):
        return pl.ds(pl.multiple_of(t * SKEW, 8), CH)

    def positions(t):
        return pl.ds(pl.multiple_of(t * LANES, LANES), LANES)

    def start_state(t):
        same = jnp.broadcast_to(same_chain[pl.ds(t, 1), :], (CH, LANES)) > 0.5
        return x_ref[positions(t), :].astype(F32).T + jnp.where(same, embed_t[1], embed_t[0])

    def norm(value):
        center = value - jnp.sum(value, axis=0, keepdims=True) * (1.0 / CH)
        spread = jnp.sum(center * center, axis=0, keepdims=True) * (1.0 / CH)
        return (center * lax.rsqrt(spread + EPSILON)).astype(BF16)

    def operand(update, side, tiles, units):
        weights = ab_t[update, side * 2 * CH : (side + 1) * 2 * CH, :]
        both = jnp.dot(weights, jnp.concatenate(units, axis=1), preferred_element_type=F32)
        for k, t in enumerate(tiles):
            one = both[:, k * LANES : (k + 1) * LANES]
            stages[side][tile_at(t), :] = sigmoid(one[:CH]) * one[CH:] * pair_mask[pl.ds(t, 1), :]

    def for_tiles(begin, end, visit):
        def turn(n, carry):
            visit([begin + n * 4 + k for k in range(4)])
            return carry

        turns = (end - begin) // 4
        lax.fori_loop(0, turns, turn, 0)
        if begin + turns * 4 < end:
            visit(list(range(begin + turns * 4, end)))

    def send(number, row_to, col_to):
        pltpu.make_async_remote_copy(
            outs[number].at[row_to * 8 + col_to], ins[number].at[me],
            send_sem.at[number], recv_sem.at[number], device_id=(row_to, col_to), device_id_type=MESH,
        ).start()

    def staged(side, channel, begin, count):
        return stages[side][pl.ds(begin * SKEW + channel, count, stride=SKEW), :]

    def relay(make):
        def one(step):
            row_to, col_to = peer(step, row, col)
            channel = row_to * 8 + col_to
            for number, value in make(channel):
                outs[number][channel] = value.astype(BF16)
                send(number, row_to, col_to)

        for_each_peer(one)
        for number, value in make(me):
            ins[number][me] = value.astype(BF16)

    def arrive(*numbers):
        for number in numbers:
            others = ins[number].at[pl.ds(0, 127)]
            pltpu.make_async_copy(others, others, recv_sem.at[number]).wait()

    def give(*numbers):
        def one(step):
            row_to, col_to = peer(step, row, col)
            for number in numbers:
                send(number, row_to, col_to)

        for_each_peer(one)
        for number in numbers:
            ins[number][me] = outs[number][me]

    def got(number, source):
        return ins[number][source].astype(F32)

    def columns(visit):
        def turn(s, carry):
            visit(s, pl.ds(pl.multiple_of(s * LANES, LANES), LANES))
            return carry

        lax.fori_loop(0, 8, turn, 0)

    def wide(visit):
        def turn(n, carry):
            visit(n, pl.ds(pl.multiple_of(n * WIDE, WIDE), WIDE))
            return carry

        lax.fori_loop(0, 8 * LANES // WIDE, turn, 0)

    def wide_and_send(visit, number):
        def turn(n, carry):
            n = lax.rem(n + row, 8 * LANES // WIDE)
            visit(n, pl.ds(pl.multiple_of(n * WIDE, WIDE), WIDE))
            for i in range(16):
                for k in range(WIDE // LANES):
                    row_to = lax.rem(row + 5 * i, 16)
                    col_to = n * (WIDE // LANES) + lax.rem(col + k, 2)
                    if i == 0 and k == 0:
                        pl.when(row_to * 8 + col_to != me)(lambda: send(number, row_to, col_to))
                    else:
                        send(number, row_to, col_to)
            return carry

        lax.fori_loop(0, 8 * LANES // WIDE, turn, 0)
        ins[number][me] = outs[number][me]

    def unfolded(r, begin, end):
        return [unfold(flat[r, 7 * g : 7 * g + GROUP]) for g in range(begin, end)]

    def folded(slot, begin, rows):
        for g in range(rows.shape[0] // GROUP):
            at = 7 * (begin + g)
            flat_product[slot, at : at + GROUP] = fold(rows[g * GROUP : (g + 1) * GROUP])

    def mix(begin, count, tile_of):
        padded = -(-count // GROUP) * GROUP

        def add(c, carry):
            tile = tile_of(c)
            products[c, :padded] = tile
            return carry + tile

        empty = jnp.zeros((padded, LANES), F32)
        mean = lax.fori_loop(0, CH, add, empty, unroll=8) * (1.0 / CH)

        def add_square(c, carry):
            center = products[c, :padded] - mean
            return carry + center * center

        spread = lax.fori_loop(0, CH, add_square, empty, unroll=8) * (1.0 / CH)
        scale = lax.rsqrt(spread + EPSILON)

        def put(c, carry):
            value = (products[c, :padded] - mean) * scale
            left_stage[pl.ds(begin * SKEW + c, count, stride=SKEW), :] = value[:count]
            return carry

        lax.fori_loop(0, CH, put, 0, unroll=8)

    def got_with_row(number, extra, c):
        return jnp.concatenate([got(number, c), jnp.broadcast_to(got(extra, c)[0:1], (GROUP, LANES))], axis=0)

    def changed(update, tiles):
        mixed = jnp.concatenate([left_stage[tile_at(t), :].astype(BF16) for t in tiles], axis=1)
        change = jnp.dot(final_t[update], mixed, preferred_element_type=F32)
        return [
            state[t] + gating[t] * change[:, k * LANES : (k + 1) * LANES] for k, t in enumerate(tiles)
        ]

    def first(update, sides):
        def visit(tiles):
            values = [start_state(t) for t in tiles] if update == 0 else changed(0, tiles)
            units = [norm(value) for value in values]
            for t, value, unit in zip(tiles, values, units):
                state[t] = value
                normed[t] = unit
            for side in sides:
                operand(update, side, tiles, units)

        return visit

    def second(update):
        def visit(tiles):
            operand(update, LEFT, tiles, [normed[t] for t in tiles])

        return visit

    def third(update):
        def visit(tiles):
            units = jnp.concatenate([normed[t] for t in tiles], axis=1)
            gates = sigmoid(jnp.dot(gate_t[update], units, preferred_element_type=F32))
            for k, t in enumerate(tiles):
                gating[t] = gates[:, k * LANES : (k + 1) * LANES]

        return visit

    def last(tiles):
        for t, value in zip(tiles, changed(1, tiles)):
            out_ref[positions(t), :] = value.T.astype(BF16)

    copies["ab1"].wait()
    turn_ab(0, ab1_ref, RIGHT)
    copies["embed"].wait()
    for kind in range(2):
        embed_t[kind] = jnp.broadcast_to(embed_ref[kind : kind + 1, :], (CH, CH)).T
    x_copies[0].wait()
    for_tiles(0, FIRST, first(0, [RIGHT]))

    def right_early(channel):
        return [(RA, staged(RIGHT, channel, 0, FIRST))]

    def right_late(channel):
        return [(RB, staged(RIGHT, channel, FIRST, 24))]

    def left_early(channel):
        tile = staged(LEFT, channel, 0, 32)
        last_right = jnp.broadcast_to(staged(RIGHT, channel, TILES - 1, 1), (GROUP, LANES))
        end = jnp.where(row_of == 7, last_right, tile[24:])
        return [(LA, jnp.concatenate([tile[:24], end], axis=0))]

    def left_late(channel):
        return [(LB, staged(LEFT, channel, 31, 16)), (LX, staged(LEFT, channel, 47, 2))]

    pl.semaphore_wait(barrier, 127)
    relay(right_early)
    x_copies[1].wait()
    for_tiles(FIRST, TILES, first(0, [RIGHT]))
    relay(right_late)
    turn_ab(0, ab1_ref, LEFT)
    for_tiles(0, TILES, second(0))
    relay(left_early)
    relay(left_late)
    for name in ("gate1", "final1", "ab2", "gate2", "final2"):
        copies[name].wait()
    for update, (gate, final) in enumerate(((gate1_ref, final1_ref), (gate2_ref, final2_ref))):
        gate_t[update] = turned(gate[...])
        final_t[update] = turned(final[...])
    for side in (LEFT, RIGHT):
        turn_ab(1, ab2_ref, side)
    for_tiles(0, TILES, third(0))

    def right_columns_most(s, at):
        for r in range(16):
            source = r * 8 + s
            flat[r, 0:24] = got(RA, source)
            flat[r, 24:48] = got(RB, source)
            rows = [jnp.where(lanes < COLS, part, 0.0) for part in unfolded(r, 0, 6)]
            top = (r // 2) * LANES + (r % 2) * ROWS
            total[top : top + 48, at] = jnp.concatenate(rows, axis=0)

    def right_columns(s, at):
        rows = []
        for r in range(16):
            source = r * 8 + s
            flat[r, 40:48] = got(RB, source)[16:]
            flat[r, 48:49] = got(LA, source)[31:]
            top = (r // 2) * LANES + (r % 2) * ROWS
            rows += [total[top : top + 48, at], jnp.where(lanes < COLS, unfolded(r, 6, 7)[0], 0.0)]
        empty = jnp.zeros((LANES - 2 * ROWS, LANES), F32)
        for a in range(8):
            panel = jnp.concatenate(rows[4 * a : 4 * a + 4] + [empty], axis=0)
            right_panel[a * LANES : (a + 1) * LANES, at] = panel.astype(BF16)

    def left_columns_first(s, at):
        rows = []
        for r in range(16):
            flat[r, 0:32] = got(LA, r * 8 + s)
            rows += unfolded(r, 0, 4)
        left_panel[:512, at] = jnp.concatenate(rows, axis=0).astype(BF16)

    def left_columns_second(s, at):
        rows = []
        for r in range(16):
            source = r * 8 + s
            flat[r, 24:32] = got(LA, source)[24:]
            flat[r, 31:47] = got(LB, source)
            flat[r, 47:49] = got(LX, source)
            rows += unfolded(r, 4, 7)
        left_panel[512:896, at] = jnp.concatenate(rows, axis=0).astype(BF16)

    def outgoing_product(begin, end, half):
        count = (end - begin) // 16

        def visit(n, at):
            part = lax.dot_general(
                left_panel[begin:end, :], right_panel[at, :], (((1,), (1,)), ((), ())),
                preferred_element_type=F32,
            )
            for r in range(16):
                for k in range(WIDE // LANES):
                    block = part[r * count : (r + 1) * count, k * LANES : (k + 1) * LANES]
                    dest = r * 8 + n * (WIDE // LANES) + k
                    slot = r * 2 + k
                    if half == 0:
                        folded(slot, 0, block)
                        outs[PA][dest] = flat_product[slot, 0:24].astype(BF16)
                        kept[dest] = flat_product[slot, 24:32]
                    else:
                        flat_product[slot, 24:32] = kept[dest]
                        folded(slot, 4, block)
                        outs[PB][dest] = flat_product[slot, 24:48].astype(BF16)
                        outs[PX][dest] = flat_product[slot, 48:50].astype(BF16)

        if half == 0:
            wide_and_send(visit, PA)
        else:
            wide(visit)

    arrive(RA, RB)
    columns(right_columns_most)
    arrive(LA)
    columns(right_columns)
    columns(left_columns_first)
    outgoing_product(0, 512, 0)
    arrive(LB, LX)
    columns(left_columns_second)
    outgoing_product(512, 896, 1)
    give(PB, PX)

    def both(number, begin, count):
        return lambda channel: [
            (number, jnp.concatenate([staged(side, channel, begin, count) for side in (RIGHT, LEFT)], axis=0))
        ]

    def rest(channel):
        extra = [staged(side, channel, TILES - 1, 1) for side in (RIGHT, LEFT)]
        return both(QC, SECOND, 8)(channel) + [(QX, jnp.concatenate(extra, axis=0))]

    arrive(PA)
    mix(0, 24, lambda c: got(PA, c))
    for_tiles(0, FIRST, first(1, [RIGHT]))
    relay(lambda channel: [(QRA, staged(RIGHT, channel, 0, FIRST))])
    for_tiles(0, FIRST, second(1))
    relay(lambda channel: [(QLA, staged(LEFT, channel, 0, FIRST))])
    arrive(PB, PX)
    mix(24, 25, lambda c: got_with_row(PB, PX, c))
    for_tiles(FIRST, SECOND, first(1, [RIGHT, LEFT]))
    relay(both(QB, FIRST, 16))
    for_tiles(SECOND, TILES, first(1, [RIGHT, LEFT]))
    relay(rest)

    def incoming_columns(begin, end, numbers):
        depth = pl.ds(16 * begin, 16 * (end - begin))

        def visit(s, at):
            both_rows = [], []
            for r in range(16):
                source = r * 8 + s
                for k, side in enumerate((RIGHT, LEFT)):
                    slot = r + 16 * k
                    for top, number in numbers:
                        count = MESSAGES[number] // 2
                        if number == QX:
                            flat[slot, top : top + 1] = got(QX, source)[k : k + 1]
                        elif number == QRA:
                            flat[slot, top : top + FIRST] = got((QRA, QLA)[k], source)
                        else:
                            flat[slot, top : top + count] = got(number, source)[k * count : (k + 1) * count]
                    both_rows[k].extend(unfolded(slot, begin // GROUP, end // GROUP))
            right_panel[depth, at] = jnp.concatenate(both_rows[0], axis=0).astype(BF16)
            left_panel[at, depth] = jnp.concatenate(both_rows[1], axis=0).T.astype(BF16)

        columns(visit)

    def incoming_part(begin, end, at):
        return jnp.dot(left_panel[:, begin:end], right_panel[begin:end, at], preferred_element_type=F32)

    def incoming_first(n, at):
        total[:, at] = incoming_part(0, 384, at)

    def incoming_second(n, at):
        total[:, at] += incoming_part(384, 640, at)

    def incoming_third(n, at):
        part = total[:, at] + incoming_part(640, 896, at)
        for r in range(16):
            top = (r // 2) * LANES + (r % 2) * ROWS
            for k in range(WIDE // LANES):
                dest = r * 8 + n * (WIDE // LANES) + k
                slot = r * 2 + k
                folded(slot, 0, part[top : top + ROWS, k * LANES : (k + 1) * LANES])
                outs[QPA][dest] = flat_product[slot, 0:24].astype(BF16)
                outs[QPB][dest] = flat_product[slot, 24:40].astype(BF16)
                outs[QPC][dest] = flat_product[slot, 40:48].astype(BF16)
                outs[QPX][dest] = flat_product[slot, 48:50].astype(BF16)

    arrive(QRA, QLA)
    incoming_columns(0, 24, [(0, QRA)])
    wide(incoming_first)
    arrive(QB)
    incoming_columns(24, 40, [(0, QRA), (24, QB)])
    wide(incoming_second)
    arrive(QC, QX)
    incoming_columns(40, 56, [(24, QB), (40, QC), (48, QX)])
    wide_and_send(incoming_third, QPA)
    give(QPB)
    give(QPC, QPX)
    for_tiles(0, TILES, third(1))

    arrive(QPA)
    mix(0, 24, lambda c: got(QPA, c))
    for_tiles(0, FIRST, last)
    out_copies[0].start()
    arrive(QPB)
    mix(24, 16, lambda c: got(QPB, c))
    for_tiles(FIRST, SECOND, last)
    out_copies[1].start()
    arrive(QPC, QPX)
    mix(40, 9, lambda c: got_with_row(QPC, QPX, c))
    for_tiles(SECOND, TILES, last)
    out_copies[2].start()

    for number in range(len(MESSAGES)):
        others = outs[number].at[pl.ds(0, 127)]
        pltpu.make_async_copy(others, others, send_sem.at[number]).wait()
    for copy in out_copies:
        copy.wait()


def body(pair_repr, *args):
    messages = [pltpu.VMEM((CH, count, LANES), BF16) for count in MESSAGES]
    flat_shape = (TILES * LANES, CH)
    held = [pltpu.VMEM(flat_shape, BF16)]
    for number, arg in enumerate(args):
        held.append((pltpu.SMEM if number < 2 else pltpu.VMEM)(arg.shape, arg.dtype))
    out = pl.pallas_call(
        kernel,
        out_shape=pltpu.VMEM(flat_shape, BF16),
        in_specs=[pl.BlockSpec(memory_space=pltpu.HBM)] * 10,
        out_specs=pl.BlockSpec(memory_space=pl.ANY),
        scratch_shapes=[
            *held,
            pltpu.VMEM(flat_shape, BF16),
            pltpu.VMEM((TILES, CH, LANES), F32),
            pltpu.VMEM((TILES, CH, LANES), BF16),
            pltpu.VMEM((TILES, CH, LANES), F32),
            pltpu.VMEM((TILES * SKEW, LANES), F32),
            pltpu.VMEM((TILES * SKEW, LANES), F32),
            pltpu.VMEM((ROWS, LANES), F32),
            pltpu.VMEM((ROWS, LANES), F32),
            pltpu.VMEM((2, CH, LANES), F32),
            pltpu.VMEM((2, 4 * CH, CH), BF16),
            pltpu.VMEM((2, CH, CH), BF16),
            pltpu.VMEM((2, CH, CH), BF16),
            pltpu.VMEM((8 * LANES, 8 * LANES), BF16),
            pltpu.VMEM((8 * LANES, 8 * LANES), BF16),
            pltpu.VMEM((8 * LANES, 8 * LANES), F32),
            pltpu.VMEM((CH, GROUP, LANES), F32),
            pltpu.VMEM((CH, 32, LANES), F32),
            pltpu.VMEM((32, 56, LANES), F32),
            pltpu.VMEM((32, 56, LANES), F32),
            *messages,
            *messages,
            pltpu.SemaphoreType.DMA((len(MESSAGES),)),
            pltpu.SemaphoreType.DMA((len(MESSAGES),)),
            pltpu.SemaphoreType.DMA((11,)),
            pltpu.SemaphoreType.DMA((3,)),
        ],
        compiler_params=pltpu.CompilerParams(
            collective_id=0, has_side_effects=True, vmem_limit_bytes=56 << 20
        ),
    )(*(pltpu.with_memory_space_constraint(a, pltpu.HBM) for a in (pair_repr.reshape(flat_shape), *args)))
    return out.reshape(pair_repr.shape)


def solution(mesh):
    in_specs = (P("row", "col", None), P(), P(), P(), P(), P(), P(), P(), P(), P())
    out_specs = P("row", "col", None)
    return jax.shard_map(body, mesh=mesh, in_specs=in_specs, out_specs=out_specs, check_vma=False)
```
